32 devices in a mesh: grp: 4 (over y, core), seq: 8 (over z, x).
Axes of the slice: x: 2, y: 2, z: 4, core: 2. Of those that a mesh axis runs over, the one named last changes fastest.
Arguments:
- queries: bfloat16 [4096, 2048], P(('grp', 'seq')), may hold values from -4.5 to 4.5
- keys: bfloat16 [4096, 2048], P(('grp', 'seq')), may hold values from -4.5 to 4.5
- values: bfloat16 [4096, 2048], P(('grp', 'seq')), may hold values from -6 to 6
Outputs:
- attended: bfloat16 [4096, 2048], P(('grp', 'seq'))
The draws below stay inside these ranges and needn't reach their ends.
All inputs are finite; a program needn't handle non-finite values.
Results may differ from the reference program's by a relative error of at most 0.0034.
Values may be sent and summed in bfloat16 or wider, within the bound.
A program may use at most 64 MiB of HBM per device.

```python
import math
import jax
import jax.numpy as jnp
from jax import lax

HEADS = 16
HEAD_DIM = 128
D = 2048
BLOCK = 128
MID_ROWS = 16
TOK_DEV = 128
FAR_ROWS = 512
GROUP_ROWS = 1024
TOKENS = 4096
N_GRP = 4
N_SEQ = 8


def layered_parts(key, middle_scale, distant_scale):
    key_mid, key_far = jax.random.split(key, 2)
    outer = TOKENS // FAR_ROWS
    inner = FAR_ROWS // MID_ROWS
    middle = jax.random.normal(key_mid, (outer, inner, 1, D), jnp.float32) * middle_scale
    distant = jax.random.normal(key_far, (outer, 1, 1, D), jnp.float32) * distant_scale
    return middle + distant


def rough_part(key, spread):
    return jax.random.normal(key, (TOKENS // FAR_ROWS, FAR_ROWS // MID_ROWS, MID_ROWS, D), jnp.float32) * spread


def draw_queries(key, part):
    key = jax.random.fold_in(key, 11)
    key_rough, key_smooth = jax.random.split(key, 2)
    field = rough_part(key_rough, 0.8)
    field = (field + layered_parts(key_smooth, 0.6, 1.0)).reshape(TOKENS, D)
    return jnp.clip(field, -4.5, 4.5).astype(jnp.bfloat16)


def draw_keys(key, part):
    key = jax.random.fold_in(key, 12)
    key_rough, key_smooth = jax.random.split(key, 2)
    field = rough_part(key_rough, 0.8)
    field = (field + layered_parts(key_smooth, 0.6, 1.0)).reshape(TOKENS, D)
    return jnp.clip(field, -4.5, 4.5).astype(jnp.bfloat16)


def draw_values(key, part):
    key = jax.random.fold_in(key, 13)
    key_rough, key_smooth = jax.random.split(key, 2)
    field = rough_part(key_rough, 1.0)
    field = (field + layered_parts(key_smooth, 0.7, 0.7)).reshape(TOKENS, D)
    return jnp.clip(field, -6.0, 6.0).astype(jnp.bfloat16)


def setup_inputs(seed: int = 0) -> dict:
    splits = jax.random.split(jax.random.key(seed), 4)
    queries = draw_queries(jax.random.fold_in(splits[3], 71), 0)
    keys = draw_keys(jax.random.fold_in(splits[3], 71), 0)
    values = draw_values(jax.random.fold_in(splits[3], 71), 0)
    return dict(queries=queries, keys=keys, values=values)


def run_mean(array, run):
    lead = array.shape[:-2]
    rows = array.shape[-2]
    width = array.shape[-1]
    return lax.optimization_barrier(jnp.mean(array.astype(jnp.float32).reshape(lead + (rows // run, run, width)), axis=-2))

def as_product(weights):
    rounded = lax.optimization_barrier(weights.astype(jnp.bfloat16))
    return rounded.astype(jnp.float32)

def merge_levels(query_rows, mid_query, extended, group_pair, far_pair, first, last, seat, far_allowed):
    rows = query_rows.shape[0]
    blocks = rows // BLOCK
    scale = 1.0 / math.sqrt(HEAD_DIM)
    tiled = extended.reshape(2, blocks + 2, BLOCK, HEADS, HEAD_DIM)
    window = jnp.concatenate([tiled[:, :-2], tiled[:, 1:-1], tiled[:, 2:]], axis=2).astype(jnp.float32)
    query_blocks = query_rows.reshape(blocks, BLOCK, HEADS, HEAD_DIM).astype(jnp.float32)
    near = jnp.einsum('nqhd,nkhd->nhqk', query_blocks, window[0], precision=lax.Precision.HIGHEST) * scale
    position = jnp.arange(3 * BLOCK)
    slot = jnp.arange(blocks)
    drop_left = first & (slot[:, None] == 0) & (position[None, :] < BLOCK)
    drop_right = last & (slot[:, None] == blocks - 1) & (position[None, :] >= 2 * BLOCK)
    near = jnp.where((drop_left | drop_right)[:, None, None, :], -jnp.inf, near)
    mid_local = mid_query.shape[0]
    count = group_pair.shape[1]
    ratio = BLOCK // MID_ROWS
    query_index = seat * mid_local + jnp.arange(mid_local)
    mid_allowed = jnp.abs(jnp.arange(count)[None, :] // ratio - query_index[:, None] // ratio) > 1
    query_heads = mid_query.reshape(mid_local, HEADS, HEAD_DIM)
    group_keys = group_pair[0].astype(jnp.float32).reshape(count, HEADS, HEAD_DIM)
    group_values = group_pair[1].astype(jnp.float32).reshape(count, HEADS, HEAD_DIM)
    middle = jnp.einsum('ahd,chd->ahc', query_heads, group_keys, precision=lax.Precision.HIGHEST) * scale
    middle = jnp.where(mid_allowed[:, None, :], middle, -jnp.inf)
    far_count = far_pair.shape[1]
    far_keys = far_pair[0].astype(jnp.float32).reshape(far_count, HEADS, HEAD_DIM)
    far_values = far_pair[1].astype(jnp.float32).reshape(far_count, HEADS, HEAD_DIM)
    distant = jnp.einsum('ahd,chd->ahc', query_heads, far_keys, precision=lax.Precision.HIGHEST) * scale
    distant = jnp.where(far_allowed[None, None, :], distant, -jnp.inf)
    near_top = lax.optimization_barrier(jnp.max(near, axis=-1)).transpose(0, 2, 1).reshape(rows, HEADS)
    mid_top = jnp.repeat(lax.optimization_barrier(jnp.max(middle, axis=-1)), MID_ROWS, axis=0)
    far_top = jnp.repeat(lax.optimization_barrier(jnp.max(distant, axis=-1)), MID_ROWS, axis=0)
    top = jnp.maximum(near_top, jnp.maximum(mid_top, far_top))
    near_weight = jnp.exp(near - top.reshape(blocks, BLOCK, HEADS).transpose(0, 2, 1)[..., None])
    near_total = lax.optimization_barrier(jnp.sum(near_weight, axis=-1)).transpose(0, 2, 1).reshape(rows, HEADS)
    near_numer = jnp.einsum('nhqk,nkhd->nqhd', as_product(near_weight), window[1], precision=lax.Precision.HIGHEST).reshape(rows, HEADS, HEAD_DIM)
    top_grouped = top.reshape(mid_local, MID_ROWS, HEADS)[..., None]
    mid_weight = jnp.exp(middle[:, None] - top_grouped).reshape(rows, HEADS, count)
    mid_total = lax.optimization_barrier(jnp.sum(mid_weight, axis=-1))
    mid_numer = jnp.einsum('rhc,chd->rhd', as_product(mid_weight), group_values, precision=lax.Precision.HIGHEST)
    far_weight = jnp.exp(distant[:, None] - top_grouped).reshape(rows, HEADS, far_count)
    far_total = lax.optimization_barrier(jnp.sum(far_weight, axis=-1))
    far_numer = jnp.einsum('rhc,chd->rhd', as_product(far_weight), far_values, precision=lax.Precision.HIGHEST)
    result = (near_numer + mid_numer + far_numer) / (near_total + mid_total + far_total)[..., None]
    return result.reshape(rows, D).astype(jnp.bfloat16)

def reference(queries, keys, values):
    paired = jnp.stack([keys, values], axis=0)
    mid_query = run_mean(queries, MID_ROWS)
    mid_pair = run_mean(paired, MID_ROWS).astype(jnp.bfloat16)
    far_pair = run_mean(mid_pair, FAR_ROWS // MID_ROWS).astype(jnp.bfloat16)
    padded = jnp.pad(paired, ((0, 0), (BLOCK, BLOCK), (0, 0)))
    shards = N_GRP * N_SEQ
    per_group = GROUP_ROWS // MID_ROWS
    mid_local = TOK_DEV // MID_ROWS
    far_group = jnp.arange(far_pair.shape[1], dtype=jnp.int32) * FAR_ROWS // GROUP_ROWS

    def one_shard(index):
        start = (index * TOK_DEV).astype(jnp.int32)
        query_rows = lax.dynamic_slice_in_dim(queries, start, TOK_DEV, 0)
        extended = lax.dynamic_slice_in_dim(padded, start, TOK_DEV + 2 * BLOCK, 1)
        group = (index // N_SEQ).astype(jnp.int32)
        seat = (index % N_SEQ).astype(jnp.int32)
        group_pair = lax.dynamic_slice_in_dim(mid_pair, (group * per_group).astype(jnp.int32), per_group, 1)
        query_mid = lax.dynamic_slice_in_dim(mid_query, (index * mid_local).astype(jnp.int32), mid_local, 0)
        return merge_levels(query_rows, query_mid, extended, group_pair, far_pair, index == 0, index == shards - 1, seat, far_group != group)
    result = lax.map(one_shard, jnp.arange(shards, dtype=jnp.int32))
    return result.reshape(TOKENS, D)
```

```python
import functools
import math

import jax
import jax.numpy as jnp
from jax import lax
from jax.experimental import pallas as pl
from jax.experimental.pallas import tpu as pltpu
from jax.sharding import PartitionSpec as P

HEADS = 16
BLOCK = 128
MID_ROWS = 16
FAR_ROWS = 512
CHUNKS = 4
MESH = pl.DeviceIdType.MESH
F32 = jnp.float32
BF16 = jnp.bfloat16


def dot(a, b):
    return lax.dot_general(a, b, (((1,), (0,)), ((), ())), preferred_element_type=F32)


def dot_t(a, b):
    return lax.dot_general(a, b, (((1,), (1,)), ((), ())), preferred_element_type=F32)


def kernel(
    groups,
    seats,
    q_ref,
    k_ref,
    v_ref,
    o_ref,
    kv,
    qs,
    outs,
    mids,
    fars,
    local_sem,
    x_send,
    x_recv,
    own_send,
    own_recv,
    relay_send,
    relay_recv,
    mid_send,
    mid_recv,
    far_send,
    far_recv,
    out_send,
    out_recv,
    out_local,
):
    width = q_ref.shape[1]
    half = width // 2
    head_dim = width // HEADS
    cw = half // CHUNKS
    pairs = seats // 2
    total = groups * seats
    mid_pair = 2 * BLOCK // MID_ROWS
    mid_block = BLOCK // MID_ROWS
    mid_count = pairs * mid_pair
    far_local = mid_count * MID_ROWS // FAR_ROWS
    far_pad = fars.shape[2] // 2
    far_count = groups * far_pad
    scale = 1.0 / math.sqrt(head_dim)

    g = lax.axis_index("grp")
    s = lax.axis_index("seq")
    par = s % 2
    pair = s // 2
    place = g * seats + s
    mate = (g, s + 1 - 2 * par)
    left_place = (place + total - 2) % total
    right_place = (place + 2) % total
    left = (left_place // seats, left_place % seats)
    right = (right_place // seats, right_place % seats)
    has_left = place >= 2
    has_right = place < total - 2
    even = par == 0
    odd = par == 1
    mid_peers = [(g, (s + 2 * d) % seats) for d in range(1, pairs)]
    far_peers = [((g + d) % groups, s) for d in range(1, groups)]

    barrier = pltpu.get_barrier_semaphore()

    def greet(device):
        pl.semaphore_signal(barrier, inc=1, device_id=device, device_id_type=MESH)

    cross_left = (pair == 0) & has_left
    cross_right = (pair == pairs - 1) & has_right
    for device in [mate] + mid_peers + far_peers:
        greet(device)
    pl.when(cross_left)(lambda: greet(left))
    pl.when(cross_right)(lambda: greet(right))

    mine = par * half
    theirs = half - mine

    def cols(base, c):
        return pl.ds(pl.multiple_of(base + c * cw, 128), cw)

    def at(c):
        return pl.ds(c * cw, cw)

    def local_copies(c):
        return [
            pltpu.make_async_copy(
                k_ref.at[:, cols(mine, c)], kv.at[0, 1 + par, :, at(c)], local_sem.at[0, c]
            ),
            pltpu.make_async_copy(
                v_ref.at[:, cols(mine, c)], kv.at[1, 1 + par, :, at(c)], local_sem.at[1, c]
            ),
            pltpu.make_async_copy(
                q_ref.at[:, cols(mine, c)], qs.at[par, :, at(c)], local_sem.at[2, c]
            ),
        ]

    def remote(src, dst, send, recv, device):
        return pltpu.make_async_remote_copy(
            src_ref=src,
            dst_ref=dst,
            send_sem=send,
            recv_sem=recv,
            device_id=device,
            device_id_type=MESH,
        )

    def x_copies(c):
        targets = [
            (k_ref, kv.at[0, 1 + par, :, at(c)]),
            (v_ref, kv.at[1, 1 + par, :, at(c)]),
            (q_ref, qs.at[par, :, at(c)]),
        ]
        return [
            remote(src.at[:, cols(theirs, c)], dst, x_send.at[i, c], x_recv.at[i, c], mate)
            for i, (src, dst) in enumerate(targets)
        ]

    own_slot = 3 * (1 - par)
    relay_slot = 3 * par

    def own_copies(c, device):
        return [
            remote(
                src.at[:, cols(mine, c)],
                kv.at[i, own_slot, :, at(c)],
                own_send.at[i, c],
                own_recv.at[i, c],
                device,
            )
            for i, src in enumerate((k_ref, v_ref))
        ]

    def relay_copy(c, device):
        return remote(
            kv.at[:, 2 - par, :, at(c)],
            kv.at[:, relay_slot, :, at(c)],
            relay_send.at[c],
            relay_recv.at[c],
            device,
        )

    def mid_copies(c):
        return [
            remote(mids.at[c, pair], mids.at[c, pair], mid_send.at[d, c], mid_recv.at[d, c], peer)
            for d, peer in enumerate(mid_peers)
        ]

    def far_copies(c):
        return [
            remote(fars.at[c, g], fars.at[c, g], far_send.at[d, c], far_recv.at[d, c], peer)
            for d, peer in enumerate(far_peers)
        ]

    def out_remote(c):
        return remote(
            outs.at[1 - par, :, at(c)],
            o_ref.at[:, cols(mine, c)],
            out_send.at[c],
            out_recv.at[c],
            mate,
        )

    def out_own(c):
        return pltpu.make_async_copy(
            outs.at[par, :, at(c)], o_ref.at[:, cols(mine, c)], out_local.at[c]
        )

    def each(cond, make, act):
        @pl.when(cond)
        def _():
            for copy in make():
                act(copy)

    for c in range(CHUNKS):
        for copy in local_copies(c):
            copy.start()

    @pl.when(jnp.logical_not(has_left))
    def _():
        kv[:, 0] = jnp.zeros((2, BLOCK, half), BF16)

    @pl.when(jnp.logical_not(has_right))
    def _():
        kv[:, 3] = jnp.zeros((2, BLOCK, half), BF16)

    crossing = cross_left.astype(jnp.int32) + cross_right.astype(jnp.int32)
    pl.semaphore_wait(barrier, 1 + len(mid_peers) + len(far_peers) + crossing)

    start = lambda copy: copy.start()
    for c in range(CHUNKS):
        for copy in x_copies(c):
            copy.start()
        each(even & has_left, lambda c=c: own_copies(c, left), start)
        each(odd & has_right, lambda c=c: own_copies(c, right), start)

    run = lax.broadcasted_iota(jnp.int32, (mid_pair, 2 * BLOCK), 1) // MID_ROWS
    row = lax.broadcasted_iota(jnp.int32, (mid_pair, 2 * BLOCK), 0)
    mid_mean = jnp.where(run == row, 1.0 / MID_ROWS, 0.0).astype(BF16)
    ratio = FAR_ROWS // MID_ROWS
    run = lax.broadcasted_iota(jnp.int32, (far_pad, mid_count), 1) // ratio
    row = lax.broadcasted_iota(jnp.int32, (far_pad, mid_count), 0)
    far_mean = jnp.where(run == row, 1.0 / ratio, 0.0).astype(BF16)

    shape = (mid_pair, 1, mid_count)
    query_block = 2 * pair + lax.broadcasted_iota(jnp.int32, shape, 0) // mid_block
    key_block = lax.broadcasted_iota(jnp.int32, shape, 2) // mid_block
    mid_ok = jnp.abs(key_block - query_block) > 1
    shape = (mid_pair, 1, far_count)
    far_index = lax.broadcasted_iota(jnp.int32, shape, 2)
    far_ok = (far_index // far_pad != g) & (far_index % far_pad < far_local)
    bias = jnp.concatenate(
        [jnp.where(mid_ok, 0.0, -jnp.inf), jnp.where(far_ok, 0.0, -jnp.inf)], axis=2
    )

    def arrive(c):
        for copy in local_copies(c)[:2]:
            copy.wait()
        for copy in x_copies(c)[:2]:
            copy.wait_recv()
        each(even & has_right, lambda: [relay_copy(c, right)], start)
        each(odd & has_left, lambda: [relay_copy(c, left)], start)
        for i in range(2):
            rows = kv[i, 1:3, :, at(c)].reshape(2 * BLOCK, cw)
            mids[c, pair, i * mid_pair : (i + 1) * mid_pair, :] = dot(mid_mean, rows).astype(BF16)
        for copy in mid_copies(c):
            copy.start()

    def summarise(c):
        for copy in mid_copies(c):
            copy.wait_recv()
        for i in range(2):
            rows = mids[c, :, i * mid_pair : (i + 1) * mid_pair, :].reshape(mid_count, cw)
            fars[c, g, i * far_pad : (i + 1) * far_pad, :] = dot(far_mean, rows).astype(BF16)
        for copy in far_copies(c):
            copy.start()

    def attend(c):
        local_copies(c)[2].wait()
        x_copies(c)[2].wait_recv()
        recv = lambda copy: copy.wait_recv()
        each(even & has_right, lambda: own_copies(c, left), recv)
        each(odd & has_left, lambda: own_copies(c, right), recv)
        each(even & has_left, lambda: [relay_copy(c, right)], recv)
        each(odd & has_right, lambda: [relay_copy(c, left)], recv)
        for copy in far_copies(c):
            copy.wait_recv()
        for h in range(cw // head_dim):
            near_cols = pl.ds(c * cw + h * head_dim, head_dim)
            here = pl.ds(h * head_dim, head_dim)
            side = []
            for i in range(2):
                mid = mids[c, :, i * mid_pair : (i + 1) * mid_pair, here]
                far = fars[c, :, i * far_pad : (i + 1) * far_pad, here]
                side.append(
                    jnp.concatenate(
                        [mid.reshape(mid_count, head_dim), far.reshape(far_count, head_dim)], axis=0
                    )
                )
            query = qs[:, :, near_cols].reshape(2 * BLOCK, head_dim)
            coarse = dot_t(query, side[0]).reshape(mid_pair, MID_ROWS, mid_count + far_count)
            coarse = jnp.sum(coarse, axis=1, keepdims=True) * (scale / MID_ROWS) + bias
            coarse = jnp.broadcast_to(coarse, (mid_pair, MID_ROWS, mid_count + far_count))
            coarse = coarse.reshape(2 * BLOCK, mid_count + far_count)
            for j in range(2):
                rows = slice(j * BLOCK, (j + 1) * BLOCK)
                keys = kv[0, j : j + 3, :, near_cols].reshape(3 * BLOCK, head_dim)
                vals = kv[1, j : j + 3, :, near_cols].reshape(3 * BLOCK, head_dim)
                near = dot_t(query[rows], keys) * scale
                if j == 0:
                    edge = jnp.where(has_left, near[:, :BLOCK], -jnp.inf)
                    near = jnp.concatenate([edge, near[:, BLOCK:]], axis=1)
                else:
                    edge = jnp.where(has_right, near[:, 2 * BLOCK :], -jnp.inf)
                    near = jnp.concatenate([near[:, : 2 * BLOCK], edge], axis=1)
                scores = jnp.concatenate([near, coarse[rows]], axis=1)
                weight = jnp.exp(scores - jnp.max(scores, axis=1, keepdims=True))
                norm = jnp.sum(weight, axis=1, keepdims=True)
                numer = dot(weight.astype(BF16), jnp.concatenate([vals, side[1]], axis=0))
                outs[j, :, near_cols] = (numer * (1.0 / norm)).astype(BF16)
        out_remote(c).start()
        out_own(c).start()

    for t in range(CHUNKS + 2):
        if t < CHUNKS:
            arrive(t)
        if 1 <= t <= CHUNKS:
            summarise(t - 1)
        if t >= 2:
            attend(t - 2)

    sent = lambda copy: copy.wait_send()
    for c in range(CHUNKS):
        for copy in x_copies(c) + mid_copies(c) + far_copies(c):
            copy.wait_send()
        each(even & has_left, lambda: own_copies(c, left), sent)
        each(odd & has_right, lambda: own_copies(c, right), sent)
        each(even & has_right, lambda: [relay_copy(c, right)], sent)
        each(odd & has_left, lambda: [relay_copy(c, left)], sent)
        out_own(c).wait()
        out_remote(c).wait_send()
        out_remote(c).wait_recv()


def per_device(groups, seats, queries, keys, values):
    rows, width = queries.shape
    half = width // 2
    cw = half // CHUNKS
    pairs = seats // 2
    mid_pair = 2 * BLOCK // MID_ROWS
    far_local = pairs * 2 * BLOCK // FAR_ROWS
    far_pad = -(-far_local // 16) * 16
    dma = pltpu.SemaphoreType.DMA
    peers = max(pairs - 1, 1)
    others = max(groups - 1, 1)
    return pl.pallas_call(
        functools.partial(kernel, groups, seats),
        out_shape=jax.ShapeDtypeStruct((rows, width), BF16),
        in_specs=[pl.BlockSpec(memory_space=pl.ANY)] * 3,
        out_specs=pl.BlockSpec(memory_space=pl.ANY),
        scratch_shapes=[
            pltpu.VMEM((2, 4, BLOCK, half), BF16),
            pltpu.VMEM((2, BLOCK, half), BF16),
            pltpu.VMEM((2, BLOCK, half), BF16),
            pltpu.VMEM((CHUNKS, pairs, 2 * mid_pair, cw), BF16),
            pltpu.VMEM((CHUNKS, groups, 2 * far_pad, cw), BF16),
            dma((3, CHUNKS)),
            dma((3, CHUNKS)),
            dma((3, CHUNKS)),
            dma((2, CHUNKS)),
            dma((2, CHUNKS)),
            dma((CHUNKS,)),
            dma((CHUNKS,)),
            dma((peers, CHUNKS)),
            dma((peers, CHUNKS)),
            dma((others, CHUNKS)),
            dma((others, CHUNKS)),
            dma((CHUNKS,)),
            dma((CHUNKS,)),
            dma((CHUNKS,)),
        ],
        compiler_params=pltpu.CompilerParams(collective_id=0, has_side_effects=True),
    )(queries, keys, values)


def solution(mesh):
    groups, seats = mesh.shape["grp"], mesh.shape["seq"]
    spec = P(("grp", "seq"), None)
    return jax.shard_map(
        functools.partial(per_device, groups, seats),
        mesh=mesh,
        in_specs=(spec, spec, spec),
        out_specs=spec,
        check_vma=False,
    )
```

```python
import functools
import math

import jax
import jax.numpy as jnp
from jax import lax
from jax.experimental import pallas as pl
from jax.experimental.pallas import tpu as pltpu
from jax.sharding import PartitionSpec as P

HEADS = 16
BLOCK = 128
MID_ROWS = 16
FAR_ROWS = 512
CHUNKS = 4
DEPTH = 2
MESH = pl.DeviceIdType.MESH
F32 = jnp.float32
BF16 = jnp.bfloat16


def dot(a, b):
    return lax.dot_general(a, b, (((1,), (0,)), ((), ())), preferred_element_type=F32)


def dot_t(a, b):
    return lax.dot_general(a, b, (((1,), (1,)), ((), ())), preferred_element_type=F32)


def kernel(
    groups,
    seats,
    q_ref,
    k_ref,
    v_ref,
    o_ref,
    kv,
    qs,
    outs,
    rest,
    rest_mid,
    mids,
    fars,
    side,
    local_sem,
    rest_send,
    rest_recv,
    x_send,
    x_recv,
    own_send,
    own_recv,
    relay_send,
    relay_recv,
    mid_send,
    mid_recv,
    far_send,
    far_recv,
    out_send,
    out_recv,
    out_local,
):
    width = q_ref.shape[1]
    half = width // 2
    head_dim = width // HEADS
    cw = half // CHUNKS
    pairs = seats // 2
    total = groups * seats
    mid_pair = 2 * BLOCK // MID_ROWS
    mid_block = BLOCK // MID_ROWS
    mid_count = pairs * mid_pair
    far_local = mid_count * MID_ROWS // FAR_ROWS
    far_pad = fars.shape[1] // 2
    side_count = side.shape[1]
    scale = 1.0 / math.sqrt(head_dim)

    g = lax.axis_index("grp")
    s = lax.axis_index("seq")
    par = s % 2
    pair = s // 2
    place = g * seats + s
    mate = (g, s + 1 - 2 * par)
    left_place = (place + total - 2) % total
    right_place = (place + 2) % total
    left = (left_place // seats, left_place % seats)
    right = (right_place // seats, right_place % seats)
    has_left = place >= 2
    has_right = place < total - 2
    even = par == 0
    odd = par == 1
    mid_peers = [(g, (s + 2 * d) % seats) for d in range(1, pairs)]
    far_peers = [((g + d) % groups, s) for d in range(1, groups)]

    barrier = pltpu.get_barrier_semaphore()

    def greet(device):
        pl.semaphore_signal(barrier, inc=1, device_id=device, device_id_type=MESH)

    cross_left = (pair == 0) & has_left
    cross_right = (pair == pairs - 1) & has_right
    for device in [mate] + mid_peers + far_peers:
        greet(device)
    pl.when(cross_left)(lambda: greet(left))
    pl.when(cross_right)(lambda: greet(right))

    mine = par * half
    theirs = half - mine

    def cols(base, c):
        return pl.ds(pl.multiple_of(base + c * cw, 128), cw)

    def cols_half(base):
        return pl.ds(pl.multiple_of(base, 128), half)

    def at(c):
        return pl.ds(c * cw, cw)

    local = []
    for i, (src, dst) in enumerate(
        [
            (k_ref.at[:, cols_half(mine)], kv.at[0, 1 + par]),
            (v_ref.at[:, cols_half(mine)], kv.at[1, 1 + par]),
            (k_ref.at[:, cols_half(theirs)], rest.at[0]),
            (v_ref.at[:, cols_half(theirs)], rest.at[1]),
            (q_ref.at[:, cols_half(mine)], qs.at[par]),
        ]
    ):
        local.append(pltpu.make_async_copy(src, dst, local_sem.at[i]))

    def remote(src, dst, send, recv, device):
        return pltpu.make_async_remote_copy(
            src_ref=src,
            dst_ref=dst,
            send_sem=send,
            recv_sem=recv,
            device_id=device,
            device_id_type=MESH,
        )

    def x_copies(c):
        targets = [
            (k_ref, kv.at[0, 1 + par, :, at(c)]),
            (v_ref, kv.at[1, 1 + par, :, at(c)]),
            (q_ref, qs.at[par, :, at(c)]),
        ]
        return [
            remote(src.at[:, cols(theirs, c)], dst, x_send.at[i, c], x_recv.at[i, c], mate)
            for i, (src, dst) in enumerate(targets)
        ]

    own_slot = 3 * (1 - par)
    relay_slot = 3 * par

    def own_copies(c, device):
        return [
            remote(
                src.at[:, cols(mine, c)],
                kv.at[i, own_slot, :, at(c)],
                own_send.at[i, c],
                own_recv.at[i, c],
                device,
            )
            for i, src in enumerate((k_ref, v_ref))
        ]

    def relay_copy(c, device):
        return remote(
            kv.at[:, 2 - par, :, at(c)],
            kv.at[:, relay_slot, :, at(c)],
            relay_send.at[c],
            relay_recv.at[c],
            device,
        )

    rest_copy = remote(rest_mid, mids.at[pair, par], rest_send, rest_recv, mate)
    mid_copies = [
        remote(mids.at[pair], mids.at[pair], mid_send.at[d], mid_recv.at[d], peer)
        for d, peer in enumerate(mid_peers)
    ]
    far_copies = [
        remote(fars.at[g], fars.at[g], far_send.at[d], far_recv.at[d], peer)
        for d, peer in enumerate(far_peers)
    ]

    def out_remote(c):
        return remote(
            outs.at[1 - par, :, at(c)],
            o_ref.at[:, cols(mine, c)],
            out_send.at[c],
            out_recv.at[c],
            mate,
        )

    def out_own(c):
        return pltpu.make_async_copy(
            outs.at[par, :, at(c)], o_ref.at[:, cols(mine, c)], out_local.at[c]
        )

    def each(cond, make, act):
        @pl.when(cond)
        def _():
            for copy in make():
                act(copy)

    for copy in local:
        copy.start()

    @pl.when(jnp.logical_not(has_left))
    def _():
        kv[:, 0] = jnp.zeros((2, BLOCK, half), BF16)

    @pl.when(jnp.logical_not(has_right))
    def _():
        kv[:, 3] = jnp.zeros((2, BLOCK, half), BF16)

    def table(rows, columns):
        shape = (rows, columns)
        return (
            lax.broadcasted_iota(jnp.int32, shape, 0),
            lax.broadcasted_iota(jnp.int32, shape, 1),
        )

    row, col = table(mid_pair, 2 * BLOCK)
    mid_mean = jnp.where(col // MID_ROWS == row, 1.0 / MID_ROWS, 0.0).astype(BF16)
    for copy in local[:4]:
        copy.wait()
    mids[pair, par] = dot(mid_mean, kv[:, 1 + par].reshape(2 * BLOCK, half)).astype(BF16)
    rest_mid[...] = dot(mid_mean, rest[...].reshape(2 * BLOCK, half)).astype(BF16)

    crossing = cross_left.astype(jnp.int32) + cross_right.astype(jnp.int32)
    pl.semaphore_wait(barrier, 1 + len(mid_peers) + len(far_peers) + crossing)

    start = lambda copy: copy.start()
    start = lambda copy: copy.start()

    def push_pair(c):
        for copy in x_copies(c)[:2]:
            copy.start()
        each(even & has_left, lambda: own_copies(c, left), start)
        each(odd & has_right, lambda: own_copies(c, right), start)

    queue = [functools.partial(push_pair, c) for c in range(CHUNKS)]
    batch = CHUNKS // DEPTH
    for b in range(DEPTH):
        queue.append(
            lambda b=b: [x_copies(c)[2].start() for c in range(b * batch, (b + 1) * batch)]
        )
    rest_copy.start()
    for push in queue[:DEPTH]:
        push()
    rest_copy.wait_recv()
    for copy in mid_copies:
        copy.start()

    mid_raw = pairs * 2 * mid_pair
    far_raw = groups * 2 * far_pad
    ratio = FAR_ROWS // MID_ROWS

    def mid_place(raw):
        return raw // (2 * mid_block) * mid_block + raw % mid_block, raw // mid_block % 2

    def far_place(raw):
        return raw // (2 * far_pad) * far_pad + raw % far_pad + mid_count, raw // far_pad % 2

    row, col = table(2 * far_pad, mid_raw)
    index, kind = mid_place(col)
    far_hit = (index // ratio == row % far_pad) & (kind == row // far_pad)
    far_mean = jnp.where(far_hit, 1.0 / ratio, 0.0).astype(BF16)

    def pick(kind, place, raw):
        row, col = table(side_count, raw)
        index, found = place(col)
        return jnp.where((index == row) & (found == kind), 1.0, 0.0).astype(BF16)

    shape = (mid_pair, 1, side_count)
    query_block = 2 * pair + lax.broadcasted_iota(jnp.int32, shape, 0) // mid_block
    index = lax.broadcasted_iota(jnp.int32, shape, 2)
    far_index = index - mid_count
    mid_ok = (index < mid_count) & (jnp.abs(index // mid_block - query_block) > 1)
    far_ok = (far_index >= 0) & (far_index < groups * far_pad)
    far_ok = far_ok & (far_index // far_pad != g) & (far_index % far_pad < far_local)
    bias = jnp.where(mid_ok | far_ok, 0.0, -jnp.inf)

    def arrive(c):
        for copy in x_copies(c)[:2]:
            copy.wait_recv()
        queue[c + DEPTH]()
        each(even & has_right, lambda: [relay_copy(c, right)], start)
        each(odd & has_left, lambda: [relay_copy(c, left)], start)

    def summarise():
        for copy in mid_copies:
            copy.wait_recv()
        fars[g] = dot(far_mean, mids[...].reshape(mid_raw, half)).astype(BF16)
        for copy in far_copies:
            copy.start()

    def collect():
        for copy in far_copies:
            copy.wait_recv()
        for i in range(2):
            picked = dot(pick(i, mid_place, mid_raw), mids[...].reshape(mid_raw, half))
            picked += dot(pick(i, far_place, far_raw), fars[...].reshape(far_raw, half))
            side[i] = picked.astype(BF16)

    def attend(c):
        x_copies(c)[2].wait_recv()
        recv = lambda copy: copy.wait_recv()
        each(even & has_right, lambda: own_copies(c, left), recv)
        each(odd & has_left, lambda: own_copies(c, right), recv)
        each(even & has_left, lambda: [relay_copy(c, right)], recv)
        each(odd & has_right, lambda: [relay_copy(c, left)], recv)
        for h in range(cw // head_dim):
            near_cols = pl.ds(c * cw + h * head_dim, head_dim)
            query = qs[:, :, near_cols].reshape(2 * BLOCK, head_dim)
            coarse = dot_t(query, side[0, :, near_cols]).reshape(mid_pair, MID_ROWS, side_count)
            coarse = jnp.sum(coarse, axis=1, keepdims=True) * (scale / MID_ROWS) + bias
            coarse = jnp.broadcast_to(coarse, (mid_pair, MID_ROWS, side_count))
            coarse = coarse.reshape(2 * BLOCK, side_count)
            for j in range(2):
                rows = slice(j * BLOCK, (j + 1) * BLOCK)
                keys = kv[0, j : j + 3, :, near_cols].reshape(3 * BLOCK, head_dim)
                vals = kv[1, j : j + 3, :, near_cols].reshape(3 * BLOCK, head_dim)
                values = jnp.concatenate([vals, side[1, :, near_cols]], axis=0)
                near = dot_t(query[rows], keys) * scale
                if j == 0:
                    edge = jnp.where(has_left, near[:, :BLOCK], -jnp.inf)
                    near = jnp.concatenate([edge, near[:, BLOCK:]], axis=1)
                else:
                    edge = jnp.where(has_right, near[:, 2 * BLOCK :], -jnp.inf)
                    near = jnp.concatenate([near[:, : 2 * BLOCK], edge], axis=1)
                scores = jnp.concatenate([near, coarse[rows]], axis=1)
                weight = jnp.exp(scores - jnp.max(scores, axis=1, keepdims=True))
                norm = jnp.sum(weight, axis=1, keepdims=True)
                numer = dot(weight.astype(BF16), values)
                outs[j, :, near_cols] = (numer * (1.0 / norm)).astype(BF16)
        out_remote(c).start()
        out_own(c).start()

    for c in range(CHUNKS):
        if c == CHUNKS // 2:
            summarise()
        if c == CHUNKS - 1:
            collect()
        arrive(c)
    local[4].wait()
    for c in range(CHUNKS):
        attend(c)

    sent = lambda copy: copy.wait_send()
    for copy in [rest_copy] + mid_copies + far_copies:
        copy.wait_send()
    for c in range(CHUNKS):
        for copy in x_copies(c):
            copy.wait_send()
        each(even & has_left, lambda: own_copies(c, left), sent)
        each(odd & has_right, lambda: own_copies(c, right), sent)
        each(even & has_right, lambda: [relay_copy(c, right)], sent)
        each(odd & has_left, lambda: [relay_copy(c, left)], sent)
        out_own(c).wait()
        out_remote(c).wait_send()
        out_remote(c).wait_recv()


def per_device(groups, seats, queries, keys, values):
    rows, width = queries.shape
    half = width // 2
    pairs = seats // 2
    mid_pair = 2 * BLOCK // MID_ROWS
    far_local = pairs * 2 * BLOCK // FAR_ROWS
    far_pad = -(-far_local // 8) * 8
    mid_count = pairs * mid_pair
    side_count = -(-(mid_count + groups * far_pad) // 128) * 128
    dma = pltpu.SemaphoreType.DMA
    peers = max(pairs - 1, 1)
    others = max(groups - 1, 1)
    return pl.pallas_call(
        functools.partial(kernel, groups, seats),
        out_shape=jax.ShapeDtypeStruct((rows, width), BF16),
        in_specs=[pl.BlockSpec(memory_space=pl.ANY)] * 3,
        out_specs=pl.BlockSpec(memory_space=pl.ANY),
        scratch_shapes=[
            pltpu.VMEM((2, 4, BLOCK, half), BF16),
            pltpu.VMEM((2, BLOCK, half), BF16),
            pltpu.VMEM((2, BLOCK, half), BF16),
            pltpu.VMEM((2, BLOCK, half), BF16),
            pltpu.VMEM((mid_pair, half), BF16),
            pltpu.VMEM((pairs, 2, mid_pair, half), BF16),
            pltpu.VMEM((groups, 2 * far_pad, half), BF16),
            pltpu.VMEM((2, side_count, half), BF16),
            dma((5,)),
            dma(()),
            dma(()),
            dma((3, CHUNKS)),
            dma((3, CHUNKS)),
            dma((2, CHUNKS)),
            dma((2, CHUNKS)),
            dma((CHUNKS,)),
            dma((CHUNKS,)),
            dma((peers,)),
            dma((peers,)),
            dma((others,)),
            dma((others,)),
            dma((CHUNKS,)),
            dma((CHUNKS,)),
            dma((CHUNKS,)),
        ],
        compiler_params=pltpu.CompilerParams(collective_id=0, has_side_effects=True),
    )(queries, keys, values)


def solution(mesh):
    groups, seats = mesh.shape["grp"], mesh.shape["seq"]
    spec = P(("grp", "seq"), None)
    return jax.shard_map(
        functools.partial(per_device, groups, seats),
        mesh=mesh,
        in_specs=(spec, spec, spec),
        out_specs=spec,
        check_vma=False,
    )
```

```python
import functools
import math

import jax
import jax.numpy as jnp
from jax import lax
from jax.experimental import pallas as pl
from jax.experimental.pallas import tpu as pltpu
from jax.sharding import PartitionSpec as P

HEADS = 16
BLOCK = 128
MID_ROWS = 16
FAR_ROWS = 512
CHUNKS = 4
DEPTH = 2
MESH = pl.DeviceIdType.MESH
F32 = jnp.float32
BF16 = jnp.bfloat16


def dot(a, b):
    return lax.dot_general(a, b, (((1,), (0,)), ((), ())), preferred_element_type=F32)


def dot_t(a, b):
    return lax.dot_general(a, b, (((1,), (1,)), ((), ())), preferred_element_type=F32)


def kernel(
    groups,
    seats,
    q_ref,
    k_ref,
    v_ref,
    o_ref,
    kv,
    qs,
    outs,
    rest,
    rest_mid,
    mids,
    fars,
    side,
    local_sem,
    rest_send,
    rest_recv,
    x_send,
    x_recv,
    own_send,
    own_recv,
    relay_send,
    relay_recv,
    mid_send,
    mid_recv,
    far_send,
    far_recv,
    out_send,
    out_recv,
    out_local,
):
    width = q_ref.shape[1]
    half = width // 2
    head_dim = width // HEADS
    cw = half // CHUNKS
    pairs = seats // 2
    total = groups * seats
    mid_pair = 2 * BLOCK // MID_ROWS
    mid_block = BLOCK // MID_ROWS
    mid_count = pairs * mid_pair
    far_local = mid_count * MID_ROWS // FAR_ROWS
    far_pad = fars.shape[1] // 2
    side_count = side.shape[1]
    scale = 1.0 / math.sqrt(head_dim)

    g = lax.axis_index("grp")
    s = lax.axis_index("seq")
    par = s % 2
    pair = s // 2
    place = g * seats + s
    mate = (g, s + 1 - 2 * par)
    left_place = (place + total - 2) % total
    right_place = (place + 2) % total
    left = (left_place // seats, left_place % seats)
    right = (right_place // seats, right_place % seats)
    has_left = place >= 2
    has_right = place < total - 2
    even = par == 0
    odd = par == 1
    mid_peers = [(g, (s + 2 * d) % seats) for d in range(1, pairs)]
    far_peers = [((g + d) % groups, s) for d in range(1, groups)]

    barrier = pltpu.get_barrier_semaphore()

    def greet(device):
        pl.semaphore_signal(barrier, inc=1, device_id=device, device_id_type=MESH)

    cross_left = (pair == 0) & has_left
    cross_right = (pair == pairs - 1) & has_right
    for device in [mate] + mid_peers + far_peers:
        greet(device)
    pl.when(cross_left)(lambda: greet(left))
    pl.when(cross_right)(lambda: greet(right))

    mine = par * half
    theirs = half - mine

    def cols(base, c):
        return pl.ds(pl.multiple_of(base + c * cw, 128), cw)

    def cols_half(base):
        return pl.ds(pl.multiple_of(base, 128), half)

    def at(c):
        return pl.ds(c * cw, cw)

    local = []
    for i, (src, dst) in enumerate(
        [
            (k_ref.at[:, cols_half(mine)], kv.at[0, 1 + par]),
            (v_ref.at[:, cols_half(mine)], kv.at[1, 1 + par]),
            (k_ref.at[:, cols_half(theirs)], rest.at[0]),
            (v_ref.at[:, cols_half(theirs)], rest.at[1]),
            (q_ref.at[:, cols_half(mine)], qs.at[par]),
        ]
    ):
        local.append(pltpu.make_async_copy(src, dst, local_sem.at[i]))

    def remote(src, dst, send, recv, device):
        return pltpu.make_async_remote_copy(
            src_ref=src,
            dst_ref=dst,
            send_sem=send,
            recv_sem=recv,
            device_id=device,
            device_id_type=MESH,
        )

    def x_copies(c):
        targets = [
            (k_ref, kv.at[0, 1 + par, :, at(c)]),
            (v_ref, kv.at[1, 1 + par, :, at(c)]),
            (q_ref, qs.at[par, :, at(c)]),
        ]
        return [
            remote(src.at[:, cols(theirs, c)], dst, x_send.at[i, c], x_recv.at[i, c], mate)
            for i, (src, dst) in enumerate(targets)
        ]

    own_slot = 3 * (1 - par)
    relay_slot = 3 * par

    def own_copies(c, device):
        return [
            remote(
                src.at[:, cols(mine, c)],
                kv.at[i, own_slot, :, at(c)],
                own_send.at[i, c],
                own_recv.at[i, c],
                device,
            )
            for i, src in enumerate((k_ref, v_ref))
        ]

    def relay_copy(c, device):
        return remote(
            kv.at[:, 2 - par, :, at(c)],
            kv.at[:, relay_slot, :, at(c)],
            relay_send.at[c],
            relay_recv.at[c],
            device,
        )

    rest_copy = remote(rest_mid, mids.at[pair, par], rest_send, rest_recv, mate)
    mid_copies = [
        remote(mids.at[pair], mids.at[pair], mid_send.at[d], mid_recv.at[d], peer)
        for d, peer in enumerate(mid_peers)
    ]
    far_copies = [
        remote(fars.at[g], fars.at[g], far_send.at[d], far_recv.at[d], peer)
        for d, peer in enumerate(far_peers)
    ]

    def out_remote(c):
        return remote(
            outs.at[1 - par, :, at(c)],
            o_ref.at[:, cols(mine, c)],
            out_send.at[c],
            out_recv.at[c],
            mate,
        )

    def out_own(c):
        return pltpu.make_async_copy(
            outs.at[par, :, at(c)], o_ref.at[:, cols(mine, c)], out_local.at[c]
        )

    def each(cond, make, act):
        @pl.when(cond)
        def _():
            for copy in make():
                act(copy)

    for copy in local:
        copy.start()

    @pl.when(jnp.logical_not(has_left))
    def _():
        kv[:, 0] = jnp.zeros((2, BLOCK, half), BF16)

    @pl.when(jnp.logical_not(has_right))
    def _():
        kv[:, 3] = jnp.zeros((2, BLOCK, half), BF16)

    def table(rows, columns):
        shape = (rows, columns)
        return (
            lax.broadcasted_iota(jnp.int32, shape, 0),
            lax.broadcasted_iota(jnp.int32, shape, 1),
        )

    row, col = table(mid_pair, 2 * BLOCK)
    mid_mean = jnp.where(col // MID_ROWS == row, 1.0 / MID_ROWS, 0.0).astype(BF16)
    for copy in local[:4]:
        copy.wait()
    mids[pair, par] = dot(mid_mean, kv[:, 1 + par].reshape(2 * BLOCK, half)).astype(BF16)
    rest_mid[...] = dot(mid_mean, rest[...].reshape(2 * BLOCK, half)).astype(BF16)

    crossing = cross_left.astype(jnp.int32) + cross_right.astype(jnp.int32)
    pl.semaphore_wait(barrier, 1 + len(mid_peers) + len(far_peers) + crossing)

    start = lambda copy: copy.start()
    start = lambda copy: copy.start()

    def push_pair(c):
        for copy in x_copies(c)[:2]:
            copy.start()
        each(even & has_left, lambda: own_copies(c, left), start)
        each(odd & has_right, lambda: own_copies(c, right), start)

    queue = [functools.partial(push_pair, c) for c in range(CHUNKS)]
    batch = CHUNKS // DEPTH
    for b in range(DEPTH):
        queue.append(
            lambda b=b: [x_copies(c)[2].start() for c in range(b * batch, (b + 1) * batch)]
        )
    rest_copy.start()
    for push in queue[:DEPTH]:
        push()
    rest_copy.wait_recv()
    for copy in mid_copies:
        copy.start()

    mid_raw = pairs * 2 * mid_pair
    far_raw = groups * 2 * far_pad
    ratio = FAR_ROWS // MID_ROWS

    def mid_place(raw):
        return raw // (2 * mid_block) * mid_block + raw % mid_block, raw // mid_block % 2

    def far_place(raw):
        return raw // (2 * far_pad) * far_pad + raw % far_pad + mid_count, raw // far_pad % 2

    row, col = table(2 * far_pad, mid_raw)
    index, kind = mid_place(col)
    far_hit = (index // ratio == row % far_pad) & (kind == row // far_pad)
    far_mean = jnp.where(far_hit, 1.0 / ratio, 0.0).astype(BF16)

    def pick(kind, place, raw):
        row, col = table(side_count, raw)
        index, found = place(col)
        return jnp.where((index == row) & (found == kind), 1.0, 0.0).astype(BF16)

    shape = (mid_pair, 1, side_count)
    query_block = 2 * pair + lax.broadcasted_iota(jnp.int32, shape, 0) // mid_block
    index = lax.broadcasted_iota(jnp.int32, shape, 2)
    far_index = index - mid_count
    mid_ok = (index < mid_count) & (jnp.abs(index // mid_block - query_block) > 1)
    far_ok = (far_index >= 0) & (far_index < groups * far_pad)
    far_ok = far_ok & (far_index // far_pad != g) & (far_index % far_pad < far_local)
    bias = jnp.where(mid_ok | far_ok, 0.0, -jnp.inf)

    def arrive(c):
        for copy in x_copies(c)[:2]:
            copy.wait_recv()
        queue[c + DEPTH]()
        each(even & has_right, lambda: [relay_copy(c, right)], start)
        each(odd & has_left, lambda: [relay_copy(c, left)], start)

    def summarise():
        for copy in mid_copies:
            copy.wait_recv()
        fars[g] = dot(far_mean, mids[...].reshape(mid_raw, half)).astype(BF16)
        for copy in far_copies:
            copy.start()

    def collect():
        for copy in far_copies:
            copy.wait_recv()
        for i in range(2):
            picked = dot(pick(i, mid_place, mid_raw), mids[...].reshape(mid_raw, half))
            picked += dot(pick(i, far_place, far_raw), fars[...].reshape(far_raw, half))
            side[i] = picked.astype(BF16)

    def attend(c):
        x_copies(c)[2].wait_recv()
        recv = lambda copy: copy.wait_recv()
        each(even & has_right, lambda: own_copies(c, left), recv)
        each(odd & has_left, lambda: own_copies(c, right), recv)
        each(even & has_left, lambda: [relay_copy(c, right)], recv)
        each(odd & has_right, lambda: [relay_copy(c, left)], recv)
        for h in range(cw // head_dim):
            near_cols = pl.ds(c * cw + h * head_dim, head_dim)
            query = qs[:, :, near_cols].reshape(2 * BLOCK, head_dim)
            coarse = dot_t(query, side[0, :, near_cols]).reshape(mid_pair, MID_ROWS, side_count)
            coarse = jnp.sum(coarse, axis=1, keepdims=True) * (scale / MID_ROWS) + bias
            coarse = jnp.broadcast_to(coarse, (mid_pair, MID_ROWS, side_count))
            coarse = coarse.reshape(2 * BLOCK, side_count)
            for j in range(2):
                rows = slice(j * BLOCK, (j + 1) * BLOCK)
                keys = kv[0, j : j + 3, :, near_cols].reshape(3 * BLOCK, head_dim)
                vals = kv[1, j : j + 3, :, near_cols].reshape(3 * BLOCK, head_dim)
                values = jnp.concatenate([vals, side[1, :, near_cols]], axis=0)
                near = dot_t(query[rows], keys) * scale
                if j == 0:
                    edge = jnp.where(has_left, near[:, :BLOCK], -jnp.inf)
                    near = jnp.concatenate([edge, near[:, BLOCK:]], axis=1)
                else:
                    edge = jnp.where(has_right, near[:, 2 * BLOCK :], -jnp.inf)
                    near = jnp.concatenate([near[:, : 2 * BLOCK], edge], axis=1)
                scores = jnp.concatenate([near, coarse[rows]], axis=1)
                weight = jnp.exp(scores - jnp.max(scores, axis=1, keepdims=True))
                norm = jnp.sum(weight, axis=1, keepdims=True)
                numer = dot(weight.astype(BF16), values)
                outs[j, :, near_cols] = (numer * (1.0 / norm)).astype(BF16)
        out_remote(c).start()
        out_own(c).start()

    for c in range(CHUNKS):
        if c == CHUNKS // 2:
            summarise()
        if c == CHUNKS - 1:
            collect()
        arrive(c)
    local[4].wait()
    for c in range(CHUNKS):
        attend(c)

    sent = lambda copy: copy.wait_send()
    for copy in [rest_copy] + mid_copies + far_copies:
        copy.wait_send()
    for c in range(CHUNKS):
        for copy in x_copies(c):
            copy.wait_send()
        each(even & has_left, lambda: own_copies(c, left), sent)
        each(odd & has_right, lambda: own_copies(c, right), sent)
        each(even & has_right, lambda: [relay_copy(c, right)], sent)
        each(odd & has_left, lambda: [relay_copy(c, left)], sent)
        out_own(c).wait()
        out_remote(c).wait_send()
        out_remote(c).wait_recv()


def per_device(groups, seats, queries, keys, values):
    rows, width = queries.shape
    half = width // 2
    pairs = seats // 2
    mid_pair = 2 * BLOCK // MID_ROWS
    far_local = pairs * 2 * BLOCK // FAR_ROWS
    far_pad = -(-far_local // 8) * 8
    mid_count = pairs * mid_pair
    side_count = -(-(mid_count + groups * far_pad) // 128) * 128
    dma = pltpu.SemaphoreType.DMA
    peers = max(pairs - 1, 1)
    others = max(groups - 1, 1)
    return pl.pallas_call(
        functools.partial(kernel, groups, seats),
        out_shape=pltpu.VMEM((rows, width), BF16),
        in_specs=[pl.BlockSpec(memory_space=pl.ANY)] * 3,
        out_specs=pl.BlockSpec(memory_space=pltpu.VMEM),
        scratch_shapes=[
            pltpu.VMEM((2, 4, BLOCK, half), BF16),
            pltpu.VMEM((2, BLOCK, half), BF16),
            pltpu.VMEM((2, BLOCK, half), BF16),
            pltpu.VMEM((2, BLOCK, half), BF16),
            pltpu.VMEM((mid_pair, half), BF16),
            pltpu.VMEM((pairs, 2, mid_pair, half), BF16),
            pltpu.VMEM((groups, 2 * far_pad, half), BF16),
            pltpu.VMEM((2, side_count, half), BF16),
            dma((5,)),
            dma(()),
            dma(()),
            dma((3, CHUNKS)),
            dma((3, CHUNKS)),
            dma((2, CHUNKS)),
            dma((2, CHUNKS)),
            dma((CHUNKS,)),
            dma((CHUNKS,)),
            dma((peers,)),
            dma((peers,)),
            dma((others,)),
            dma((others,)),
            dma((CHUNKS,)),
            dma((CHUNKS,)),
            dma((CHUNKS,)),
        ],
        compiler_params=pltpu.CompilerParams(collective_id=0, has_side_effects=True),
    )(queries, keys, values)


def solution(mesh):
    groups, seats = mesh.shape["grp"], mesh.shape["seq"]
    spec = P(("grp", "seq"), None)
    return jax.shard_map(
        functools.partial(per_device, groups, seats),
        mesh=mesh,
        in_specs=(spec, spec, spec),
        out_specs=spec,
        check_vma=False,
    )
```

```python
import functools
import math

import jax
import jax.numpy as jnp
from jax import lax
from jax.experimental import pallas as pl
from jax.experimental.pallas import tpu as pltpu
from jax.sharding import PartitionSpec as P

HEADS = 16
BLOCK = 128
MID_ROWS = 16
FAR_ROWS = 512
CHUNKS = 4
DEPTH = 2
BENT = tuple(range(0, CHUNKS - 1, 2))
MESH = pl.DeviceIdType.MESH
F32 = jnp.float32
BF16 = jnp.bfloat16


def dot(a, b):
    return lax.dot_general(a, b, (((1,), (0,)), ((), ())), preferred_element_type=F32)


def dot_t(a, b):
    return lax.dot_general(a, b, (((1,), (1,)), ((), ())), preferred_element_type=F32)


def kernel(
    groups,
    seats,
    q_ref,
    k_ref,
    v_ref,
    o_ref,
    kv,
    qs,
    outs,
    rest,
    rest_mid,
    mids,
    fars,
    side,
    bent,
    bent_send,
    bent_recv,
    pass_send,
    local_sem,
    rest_send,
    rest_recv,
    x_send,
    x_recv,
    own_send,
    own_recv,
    relay_send,
    relay_recv,
    mid_send,
    mid_recv,
    far_send,
    far_recv,
    out_send,
    out_recv,
    out_local,
):
    width = q_ref.shape[1]
    half = width // 2
    head_dim = width // HEADS
    cw = half // CHUNKS
    pairs = seats // 2
    total = groups * seats
    mid_pair = 2 * BLOCK // MID_ROWS
    mid_block = BLOCK // MID_ROWS
    mid_count = pairs * mid_pair
    far_local = mid_count * MID_ROWS // FAR_ROWS
    far_pad = fars.shape[1] // 2
    side_count = side.shape[1]
    scale = 1.0 / math.sqrt(head_dim)

    g = lax.axis_index("grp")
    s = lax.axis_index("seq")
    par = s % 2
    pair = s // 2
    place = g * seats + s
    mate = (g, s + 1 - 2 * par)
    left_place = (place + total - 2) % total
    right_place = (place + 2) % total
    left = (left_place // seats, left_place % seats)
    right = (right_place // seats, right_place % seats)
    has_left = place >= 2
    has_right = place < total - 2
    even = par == 0
    odd = par == 1
    mid_peers = [(g, (s + 2 * d) % seats) for d in range(1, pairs)]
    far_peers = [((g + d) % groups, s) for d in range(1, groups)]

    cross_left = (pair == 0) & has_left
    cross_right = (pair == pairs - 1) & has_right
    bend_left = cross_left & (g % 2 == 0)
    bend_right = cross_right & (g % 2 == 1)
    via_left = ((g + groups - 1) % groups, s)
    via_right = ((g + 1) % groups, s)
    pass_left = (pair == 0) & (g % 2 == 1) & (g < groups - 1)
    pass_right = (pair == pairs - 1) & (g % 2 == 0) & (g > 0)
    end_left = (g, (s + seats - 2) % seats)
    end_right = (g, (s + 2) % seats)

    barrier = pltpu.get_barrier_semaphore()

    def greet(device):
        pl.semaphore_signal(barrier, inc=1, device_id=device, device_id_type=MESH)

    for device in [mate] + mid_peers + far_peers:
        greet(device)
    pl.when(cross_left)(lambda: greet(left))
    pl.when(cross_right)(lambda: greet(right))

    mine = par * half
    theirs = half - mine

    def cols(base, c):
        return pl.ds(pl.multiple_of(base + c * cw, 128), cw)

    def cols_half(base):
        return pl.ds(pl.multiple_of(base, 128), half)

    def at(c):
        return pl.ds(c * cw, cw)

    local = []
    for i, (src, dst) in enumerate(
        [
            (k_ref.at[:, cols_half(mine)], kv.at[0, 1 + par]),
            (v_ref.at[:, cols_half(mine)], kv.at[1, 1 + par]),
            (k_ref.at[:, cols_half(theirs)], rest.at[0]),
            (v_ref.at[:, cols_half(theirs)], rest.at[1]),
            (q_ref.at[:, cols_half(mine)], qs.at[par]),
        ]
    ):
        local.append(pltpu.make_async_copy(src, dst, local_sem.at[i]))

    def remote(src, dst, send, recv, device):
        return pltpu.make_async_remote_copy(
            src_ref=src,
            dst_ref=dst,
            send_sem=send,
            recv_sem=recv,
            device_id=device,
            device_id_type=MESH,
        )

    def x_copies(c):
        targets = [
            (k_ref, kv.at[0, 1 + par, :, at(c)]),
            (v_ref, kv.at[1, 1 + par, :, at(c)]),
            (q_ref, qs.at[par, :, at(c)]),
        ]
        return [
            remote(src.at[:, cols(theirs, c)], dst, x_send.at[i, c], x_recv.at[i, c], mate)
            for i, (src, dst) in enumerate(targets)
        ]

    own_slot = 3 * (1 - par)
    relay_slot = 3 * par

    def own_copies(c, device):
        return [
            remote(
                src.at[:, cols(mine, c)],
                kv.at[i, own_slot, :, at(c)],
                own_send.at[i, c],
                own_recv.at[i, c],
                device,
            )
            for i, src in enumerate((k_ref, v_ref))
        ]

    def relay_copy(c, device):
        return remote(
            kv.at[:, 2 - par, :, at(c)],
            kv.at[:, relay_slot, :, at(c)],
            relay_send.at[c],
            relay_recv.at[c],
            device,
        )

    def bend_own(c, device):
        return [
            remote(
                src.at[:, cols(mine, c)],
                bent.at[i, :, at(c)],
                bent_send.at[i, c],
                bent_recv.at[i, c],
                device,
            )
            for i, src in enumerate((k_ref, v_ref))
        ]

    def bend_relay(c, device):
        return [
            remote(
                kv.at[i, 2 - par, :, at(c)],
                bent.at[i, :, at(c)],
                bent_send.at[i, c],
                bent_recv.at[i, c],
                device,
            )
            for i in range(2)
        ]

    def pass_own(c, device):
        return [
            remote(
                bent.at[i, :, at(c)],
                kv.at[i, own_slot, :, at(c)],
                pass_send.at[i, c],
                own_recv.at[i, c],
                device,
            )
            for i in range(2)
        ]

    def pass_relay(c, device):
        return remote(
            bent.at[:, :, at(c)],
            kv.at[:, relay_slot, :, at(c)],
            pass_send.at[0, c],
            relay_recv.at[c],
            device,
        )

    rest_copy = remote(rest_mid, mids.at[pair, par], rest_send, rest_recv, mate)
    mid_copies = [
        remote(mids.at[pair], mids.at[pair], mid_send.at[d], mid_recv.at[d], peer)
        for d, peer in enumerate(mid_peers)
    ]
    far_copies = [
        remote(fars.at[g], fars.at[g], far_send.at[d], far_recv.at[d], peer)
        for d, peer in enumerate(far_peers)
    ]

    def out_remote(c):
        return remote(
            outs.at[1 - par, :, at(c)],
            o_ref.at[:, cols(mine, c)],
            out_send.at[c],
            out_recv.at[c],
            mate,
        )

    def out_own(c):
        return pltpu.make_async_copy(
            outs.at[par, :, at(c)], o_ref.at[:, cols(mine, c)], out_local.at[c]
        )

    def each(cond, make, act):
        @pl.when(cond)
        def _():
            for copy in make():
                act(copy)

    def own_each(c, act):
        lefts, rights = even & has_left, odd & has_right
        if c in BENT:
            each(even & bend_left, lambda: bend_own(c, via_left), act)
            each(odd & bend_right, lambda: bend_own(c, via_right), act)
            lefts = lefts & jnp.logical_not(bend_left)
            rights = rights & jnp.logical_not(bend_right)
        each(lefts, lambda: own_copies(c, left), act)
        each(rights, lambda: own_copies(c, right), act)

    def relay_each(c, act):
        lefts, rights = odd & has_left, even & has_right
        if c in BENT:
            each(odd & bend_left, lambda: bend_relay(c, via_left), act)
            each(even & bend_right, lambda: bend_relay(c, via_right), act)
            lefts = lefts & jnp.logical_not(bend_left)
            rights = rights & jnp.logical_not(bend_right)
        each(rights, lambda: [relay_copy(c, right)], act)
        each(lefts, lambda: [relay_copy(c, left)], act)

    def pass_each(c, act):
        each(even & pass_left, lambda: pass_own(c, end_left), act)
        each(odd & pass_right, lambda: pass_own(c, end_right), act)
        each(odd & pass_left, lambda: [pass_relay(c, end_left)], act)
        each(even & pass_right, lambda: [pass_relay(c, end_right)], act)

    for copy in local:
        copy.start()

    @pl.when(jnp.logical_not(has_left))
    def _():
        kv[:, 0] = jnp.zeros((2, BLOCK, half), BF16)

    @pl.when(jnp.logical_not(has_right))
    def _():
        kv[:, 3] = jnp.zeros((2, BLOCK, half), BF16)

    def table(rows, columns):
        shape = (rows, columns)
        return (
            lax.broadcasted_iota(jnp.int32, shape, 0),
            lax.broadcasted_iota(jnp.int32, shape, 1),
        )

    row, col = table(mid_pair, 2 * BLOCK)
    mid_mean = jnp.where(col // MID_ROWS == row, 1.0 / MID_ROWS, 0.0).astype(BF16)
    for copy in local[:4]:
        copy.wait()
    mids[pair, par] = dot(mid_mean, kv[:, 1 + par].reshape(2 * BLOCK, half)).astype(BF16)
    rest_mid[...] = dot(mid_mean, rest[...].reshape(2 * BLOCK, half)).astype(BF16)

    crossing = cross_left.astype(jnp.int32) + cross_right.astype(jnp.int32)
    pl.semaphore_wait(barrier, 1 + len(mid_peers) + len(far_peers) + crossing)

    start = lambda copy: copy.start()
    start = lambda copy: copy.start()

    def push_pair(c):
        for copy in x_copies(c)[:2]:
            copy.start()
        own_each(c, start)

    queue = [functools.partial(push_pair, c) for c in range(CHUNKS)]
    batch = CHUNKS // DEPTH
    for b in range(DEPTH):
        queue.append(
            lambda b=b: [x_copies(c)[2].start() for c in range(b * batch, (b + 1) * batch)]
        )
    rest_copy.start()
    for push in queue[:DEPTH]:
        push()
    rest_copy.wait_recv()
    for copy in mid_copies:
        copy.start()

    mid_raw = pairs * 2 * mid_pair
    far_raw = groups * 2 * far_pad
    ratio = FAR_ROWS // MID_ROWS

    def mid_place(raw):
        return raw // (2 * mid_block) * mid_block + raw % mid_block, raw // mid_block % 2

    def far_place(raw):
        return raw // (2 * far_pad) * far_pad + raw % far_pad + mid_count, raw // far_pad % 2

    row, col = table(2 * far_pad, mid_raw)
    index, kind = mid_place(col)
    far_hit = (index // ratio == row % far_pad) & (kind == row // far_pad)
    far_mean = jnp.where(far_hit, 1.0 / ratio, 0.0).astype(BF16)

    def pick(kind, place, raw):
        row, col = table(side_count, raw)
        index, found = place(col)
        return jnp.where((index == row) & (found == kind), 1.0, 0.0).astype(BF16)

    shape = (mid_pair, 1, side_count)
    query_block = 2 * pair + lax.broadcasted_iota(jnp.int32, shape, 0) // mid_block
    index = lax.broadcasted_iota(jnp.int32, shape, 2)
    far_index = index - mid_count
    mid_ok = (index < mid_count) & (jnp.abs(index // mid_block - query_block) > 1)
    far_ok = (far_index >= 0) & (far_index < groups * far_pad)
    far_ok = far_ok & (far_index // far_pad != g) & (far_index % far_pad < far_local)
    bias = jnp.where(mid_ok | far_ok, 0.0, -jnp.inf)

    landed = lambda copy: copy.wait_recv()

    def arrive(c):
        for copy in x_copies(c)[:2]:
            copy.wait_recv()
        queue[c + DEPTH]()
        relay_each(c, start)
        if c - 1 in BENT:
            each(pass_left | pass_right, lambda: bend_own(c - 1, via_left), landed)
            pass_each(c - 1, start)

    def summarise():
        for copy in mid_copies:
            copy.wait_recv()
        fars[g] = dot(far_mean, mids[...].reshape(mid_raw, half)).astype(BF16)
        for copy in far_copies:
            copy.start()

    def collect():
        for copy in far_copies:
            copy.wait_recv()
        for i in range(2):
            picked = dot(pick(i, mid_place, mid_raw), mids[...].reshape(mid_raw, half))
            picked += dot(pick(i, far_place, far_raw), fars[...].reshape(far_raw, half))
            side[i] = picked.astype(BF16)

    def attend(c):
        x_copies(c)[2].wait_recv()
        recv = lambda copy: copy.wait_recv()
        each(even & has_right, lambda: own_copies(c, left), recv)
        each(odd & has_left, lambda: own_copies(c, right), recv)
        each(even & has_left, lambda: [relay_copy(c, right)], recv)
        each(odd & has_right, lambda: [relay_copy(c, left)], recv)
        for h in range(cw // head_dim):
            near_cols = pl.ds(c * cw + h * head_dim, head_dim)
            query = qs[:, :, near_cols].reshape(2 * BLOCK, head_dim)
            coarse = dot_t(query, side[0, :, near_cols]).reshape(mid_pair, MID_ROWS, side_count)
            coarse = jnp.sum(coarse, axis=1, keepdims=True) * (scale / MID_ROWS) + bias
            coarse = jnp.broadcast_to(coarse, (mid_pair, MID_ROWS, side_count))
            coarse = coarse.reshape(2 * BLOCK, side_count)
            for j in range(2):
                rows = slice(j * BLOCK, (j + 1) * BLOCK)
                keys = kv[0, j : j + 3, :, near_cols].reshape(3 * BLOCK, head_dim)
                vals = kv[1, j : j + 3, :, near_cols].reshape(3 * BLOCK, head_dim)
                values = jnp.concatenate([vals, side[1, :, near_cols]], axis=0)
                near = dot_t(query[rows], keys) * scale
                if j == 0:
                    edge = jnp.where(has_left, near[:, :BLOCK], -jnp.inf)
                    near = jnp.concatenate([edge, near[:, BLOCK:]], axis=1)
                else:
                    edge = jnp.where(has_right, near[:, 2 * BLOCK :], -jnp.inf)
                    near = jnp.concatenate([near[:, : 2 * BLOCK], edge], axis=1)
                scores = jnp.concatenate([near, coarse[rows]], axis=1)
                weight = jnp.exp(scores - jnp.max(scores, axis=1, keepdims=True))
                norm = jnp.sum(weight, axis=1, keepdims=True)
                numer = dot(weight.astype(BF16), values)
                outs[j, :, near_cols] = (numer * (1.0 / norm)).astype(BF16)
        out_remote(c).start()
        out_own(c).start()

    for c in range(CHUNKS):
        if c == CHUNKS // 2:
            summarise()
        if c == CHUNKS - 1:
            collect()
        arrive(c)
    local[4].wait()
    for c in range(CHUNKS):
        attend(c)

    sent = lambda copy: copy.wait_send()
    for copy in [rest_copy] + mid_copies + far_copies:
        copy.wait_send()
    for c in range(CHUNKS):
        for copy in x_copies(c):
            copy.wait_send()
        own_each(c, sent)
        relay_each(c, sent)
        if c in BENT:
            pass_each(c, sent)
        out_own(c).wait()
        out_remote(c).wait_send()
        out_remote(c).wait_recv()


def per_device(groups, seats, queries, keys, values):
    rows, width = queries.shape
    half = width // 2
    pairs = seats // 2
    mid_pair = 2 * BLOCK // MID_ROWS
    far_local = pairs * 2 * BLOCK // FAR_ROWS
    far_pad = -(-far_local // 8) * 8
    mid_count = pairs * mid_pair
    side_count = -(-(mid_count + groups * far_pad) // 128) * 128
    dma = pltpu.SemaphoreType.DMA
    peers = max(pairs - 1, 1)
    others = max(groups - 1, 1)
    return pl.pallas_call(
        functools.partial(kernel, groups, seats),
        out_shape=pltpu.VMEM((rows, width), BF16),
        in_specs=[pl.BlockSpec(memory_space=pl.ANY)] * 3,
        out_specs=pl.BlockSpec(memory_space=pltpu.VMEM),
        scratch_shapes=[
            pltpu.VMEM((2, 4, BLOCK, half), BF16),
            pltpu.VMEM((2, BLOCK, half), BF16),
            pltpu.VMEM((2, BLOCK, half), BF16),
            pltpu.VMEM((2, BLOCK, half), BF16),
            pltpu.VMEM((mid_pair, half), BF16),
            pltpu.VMEM((pairs, 2, mid_pair, half), BF16),
            pltpu.VMEM((groups, 2 * far_pad, half), BF16),
            pltpu.VMEM((2, side_count, half), BF16),
            pltpu.VMEM((2, BLOCK, half), BF16),
            dma((2, CHUNKS)),
            dma((2, CHUNKS)),
            dma((2, CHUNKS)),
            dma((5,)),
            dma(()),
            dma(()),
            dma((3, CHUNKS)),
            dma((3, CHUNKS)),
            dma((2, CHUNKS)),
            dma((2, CHUNKS)),
            dma((CHUNKS,)),
            dma((CHUNKS,)),
            dma((peers,)),
            dma((peers,)),
            dma((others,)),
            dma((others,)),
            dma((CHUNKS,)),
            dma((CHUNKS,)),
            dma((CHUNKS,)),
        ],
        compiler_params=pltpu.CompilerParams(collective_id=0, has_side_effects=True),
    )(queries, keys, values)


def solution(mesh):
    groups, seats = mesh.shape["grp"], mesh.shape["seq"]
    spec = P(("grp", "seq"), None)
    return jax.shard_map(
        functools.partial(per_device, groups, seats),
        mesh=mesh,
        in_specs=(spec, spec, spec),
        out_specs=spec,
        check_vma=False,
    )
```

```python
import functools
import math

import jax
import jax.numpy as jnp
from jax import lax
from jax.experimental import pallas as pl
from jax.experimental.pallas import tpu as pltpu
from jax.sharding import PartitionSpec as P

HEADS = 16
BLOCK = 128
MID_ROWS = 16
FAR_ROWS = 512
CHUNKS = 8
DEPTH = 2
BENT = tuple(range(0, CHUNKS - 1, 2))
MESH = pl.DeviceIdType.MESH
F32 = jnp.float32
BF16 = jnp.bfloat16


def dot(a, b):
    return lax.dot_general(a, b, (((1,), (0,)), ((), ())), preferred_element_type=F32)


def dot_t(a, b):
    return lax.dot_general(a, b, (((1,), (1,)), ((), ())), preferred_element_type=F32)


def kernel(
    groups,
    seats,
    q_ref,
    k_ref,
    v_ref,
    o_ref,
    kv,
    qs,
    outs,
    rest,
    rest_mid,
    mids,
    fars,
    side,
    bent,
    bent_send,
    bent_recv,
    pass_send,
    local_sem,
    rest_send,
    rest_recv,
    x_send,
    x_recv,
    own_send,
    own_recv,
    relay_send,
    relay_recv,
    mid_send,
    mid_recv,
    far_send,
    far_recv,
    out_send,
    out_recv,
    out_local,
):
    width = q_ref.shape[1]
    half = width // 2
    head_dim = width // HEADS
    cw = half // CHUNKS
    pairs = seats // 2
    total = groups * seats
    mid_pair = 2 * BLOCK // MID_ROWS
    mid_block = BLOCK // MID_ROWS
    mid_count = pairs * mid_pair
    far_local = mid_count * MID_ROWS // FAR_ROWS
    far_pad = fars.shape[1] // 2
    side_count = side.shape[1]
    scale = 1.0 / math.sqrt(head_dim)

    g = lax.axis_index("grp")
    s = lax.axis_index("seq")
    par = s % 2
    pair = s // 2
    place = g * seats + s
    mate = (g, s + 1 - 2 * par)
    left_place = (place + total - 2) % total
    right_place = (place + 2) % total
    left = (left_place // seats, left_place % seats)
    right = (right_place // seats, right_place % seats)
    has_left = place >= 2
    has_right = place < total - 2
    even = par == 0
    odd = par == 1
    mid_peers = [(g, (s + 2 * d) % seats) for d in range(1, pairs)]
    far_peers = [((g + d) % groups, s) for d in range(1, groups)]

    cross_left = (pair == 0) & has_left
    cross_right = (pair == pairs - 1) & has_right
    bend_left = cross_left & (g % 2 == 0)
    bend_right = cross_right & (g % 2 == 1)
    via_left = ((g + groups - 1) % groups, s)
    via_right = ((g + 1) % groups, s)
    pass_left = (pair == 0) & (g % 2 == 1) & (g < groups - 1)
    pass_right = (pair == pairs - 1) & (g % 2 == 0) & (g > 0)
    end_left = (g, (s + seats - 2) % seats)
    end_right = (g, (s + 2) % seats)

    barrier = pltpu.get_barrier_semaphore()

    def greet(device):
        pl.semaphore_signal(barrier, inc=1, device_id=device, device_id_type=MESH)

    for device in [mate] + mid_peers + far_peers:
        greet(device)
    pl.when(cross_left)(lambda: greet(left))
    pl.when(cross_right)(lambda: greet(right))

    mine = par * half
    theirs = half - mine

    def cols(base, c):
        return pl.ds(pl.multiple_of(base + c * cw, 128), cw)

    def cols_half(base):
        return pl.ds(pl.multiple_of(base, 128), half)

    def at(c):
        return pl.ds(c * cw, cw)

    local = []
    for i, (src, dst) in enumerate(
        [
            (k_ref.at[:, cols_half(mine)], kv.at[0, 1 + par]),
            (v_ref.at[:, cols_half(mine)], kv.at[1, 1 + par]),
            (k_ref.at[:, cols_half(theirs)], rest.at[0]),
            (v_ref.at[:, cols_half(theirs)], rest.at[1]),
            (q_ref.at[:, cols_half(mine)], qs.at[par]),
        ]
    ):
        local.append(pltpu.make_async_copy(src, dst, local_sem.at[i]))

    def remote(src, dst, send, recv, device):
        return pltpu.make_async_remote_copy(
            src_ref=src,
            dst_ref=dst,
            send_sem=send,
            recv_sem=recv,
            device_id=device,
            device_id_type=MESH,
        )

    def x_copies(c):
        targets = [
            (k_ref, kv.at[0, 1 + par, :, at(c)]),
            (v_ref, kv.at[1, 1 + par, :, at(c)]),
            (q_ref, qs.at[par, :, at(c)]),
        ]
        return [
            remote(src.at[:, cols(theirs, c)], dst, x_send.at[i, c], x_recv.at[i, c], mate)
            for i, (src, dst) in enumerate(targets)
        ]

    own_slot = 3 * (1 - par)
    relay_slot = 3 * par

    def own_copies(c, device):
        return [
            remote(
                src.at[:, cols(mine, c)],
                kv.at[i, own_slot, :, at(c)],
                own_send.at[i, c],
                own_recv.at[i, c],
                device,
            )
            for i, src in enumerate((k_ref, v_ref))
        ]

    def relay_copy(c, device):
        return remote(
            kv.at[:, 2 - par, :, at(c)],
            kv.at[:, relay_slot, :, at(c)],
            relay_send.at[c],
            relay_recv.at[c],
            device,
        )

    def bend_own(c, device):
        return [
            remote(
                src.at[:, cols(mine, c)],
                bent.at[i, :, at(c)],
                bent_send.at[i, c],
                bent_recv.at[i, c],
                device,
            )
            for i, src in enumerate((k_ref, v_ref))
        ]

    def bend_relay(c, device):
        return [
            remote(
                kv.at[i, 2 - par, :, at(c)],
                bent.at[i, :, at(c)],
                bent_send.at[i, c],
                bent_recv.at[i, c],
                device,
            )
            for i in range(2)
        ]

    def pass_own(c, device):
        return [
            remote(
                bent.at[i, :, at(c)],
                kv.at[i, own_slot, :, at(c)],
                pass_send.at[i, c],
                own_recv.at[i, c],
                device,
            )
            for i in range(2)
        ]

    def pass_relay(c, device):
        return remote(
            bent.at[:, :, at(c)],
            kv.at[:, relay_slot, :, at(c)],
            pass_send.at[0, c],
            relay_recv.at[c],
            device,
        )

    rest_copy = remote(rest_mid, mids.at[pair, par], rest_send, rest_recv, mate)
    mid_copies = [
        remote(mids.at[pair], mids.at[pair], mid_send.at[d], mid_recv.at[d], peer)
        for d, peer in enumerate(mid_peers)
    ]
    far_copies = [
        remote(fars.at[g], fars.at[g], far_send.at[d], far_recv.at[d], peer)
        for d, peer in enumerate(far_peers)
    ]

    def out_remote(c):
        return remote(
            outs.at[1 - par, :, at(c)],
            o_ref.at[:, cols(mine, c)],
            out_send.at[c],
            out_recv.at[c],
            mate,
        )

    def out_own(c):
        return pltpu.make_async_copy(
            outs.at[par, :, at(c)], o_ref.at[:, cols(mine, c)], out_local.at[c]
        )

    def each(cond, make, act):
        @pl.when(cond)
        def _():
            for copy in make():
                act(copy)

    def own_each(c, act):
        lefts, rights = even & has_left, odd & has_right
        if c in BENT:
            each(even & bend_left, lambda: bend_own(c, via_left), act)
            each(odd & bend_right, lambda: bend_own(c, via_right), act)
            lefts = lefts & jnp.logical_not(bend_left)
            rights = rights & jnp.logical_not(bend_right)
        each(lefts, lambda: own_copies(c, left), act)
        each(rights, lambda: own_copies(c, right), act)

    def relay_each(c, act):
        lefts, rights = odd & has_left, even & has_right
        if c in BENT:
            each(odd & bend_left, lambda: bend_relay(c, via_left), act)
            each(even & bend_right, lambda: bend_relay(c, via_right), act)
            lefts = lefts & jnp.logical_not(bend_left)
            rights = rights & jnp.logical_not(bend_right)
        each(rights, lambda: [relay_copy(c, right)], act)
        each(lefts, lambda: [relay_copy(c, left)], act)

    def pass_each(c, act):
        each(even & pass_left, lambda: pass_own(c, end_left), act)
        each(odd & pass_right, lambda: pass_own(c, end_right), act)
        each(odd & pass_left, lambda: [pass_relay(c, end_left)], act)
        each(even & pass_right, lambda: [pass_relay(c, end_right)], act)

    for copy in local:
        copy.start()

    @pl.when(jnp.logical_not(has_left))
    def _():
        kv[:, 0] = jnp.zeros((2, BLOCK, half), BF16)

    @pl.when(jnp.logical_not(has_right))
    def _():
        kv[:, 3] = jnp.zeros((2, BLOCK, half), BF16)

    def table(rows, columns):
        shape = (rows, columns)
        return (
            lax.broadcasted_iota(jnp.int32, shape, 0),
            lax.broadcasted_iota(jnp.int32, shape, 1),
        )

    row, col = table(mid_pair, 2 * BLOCK)
    mid_mean = jnp.where(col // MID_ROWS == row, 1.0 / MID_ROWS, 0.0).astype(BF16)
    for copy in local[:4]:
        copy.wait()
    mids[pair, par] = dot(mid_mean, kv[:, 1 + par].reshape(2 * BLOCK, half)).astype(BF16)
    rest_mid[...] = dot(mid_mean, rest[...].reshape(2 * BLOCK, half)).astype(BF16)

    crossing = cross_left.astype(jnp.int32) + cross_right.astype(jnp.int32)
    pl.semaphore_wait(barrier, 1 + len(mid_peers) + len(far_peers) + crossing)

    start = lambda copy: copy.start()
    start = lambda copy: copy.start()

    def push_pair(c):
        for copy in x_copies(c)[:2]:
            copy.start()
        own_each(c, start)

    queue = [functools.partial(push_pair, c) for c in range(CHUNKS)]
    batch = CHUNKS // DEPTH
    for b in range(DEPTH):
        queue.append(
            lambda b=b: [x_copies(c)[2].start() for c in range(b * batch, (b + 1) * batch)]
        )
    rest_copy.start()
    for push in queue[:DEPTH]:
        push()
    rest_copy.wait_recv()
    for copy in mid_copies:
        copy.start()

    mid_raw = pairs * 2 * mid_pair
    far_raw = groups * 2 * far_pad
    ratio = FAR_ROWS // MID_ROWS

    def mid_place(raw):
        return raw // (2 * mid_block) * mid_block + raw % mid_block, raw // mid_block % 2

    def far_place(raw):
        return raw // (2 * far_pad) * far_pad + raw % far_pad + mid_count, raw // far_pad % 2

    row, col = table(2 * far_pad, mid_raw)
    index, kind = mid_place(col)
    far_hit = (index // ratio == row % far_pad) & (kind == row // far_pad)
    far_mean = jnp.where(far_hit, 1.0 / ratio, 0.0).astype(BF16)

    def pick(kind, place, raw):
        row, col = table(side_count, raw)
        index, found = place(col)
        return jnp.where((index == row) & (found == kind), 1.0, 0.0).astype(BF16)

    shape = (mid_pair, 1, side_count)
    query_block = 2 * pair + lax.broadcasted_iota(jnp.int32, shape, 0) // mid_block
    index = lax.broadcasted_iota(jnp.int32, shape, 2)
    far_index = index - mid_count
    mid_ok = (index < mid_count) & (jnp.abs(index // mid_block - query_block) > 1)
    far_ok = (far_index >= 0) & (far_index < groups * far_pad)
    far_ok = far_ok & (far_index // far_pad != g) & (far_index % far_pad < far_local)
    bias = jnp.where(mid_ok | far_ok, 0.0, -jnp.inf)

    landed = lambda copy: copy.wait_recv()

    def arrive(c):
        for copy in x_copies(c)[:2]:
            copy.wait_recv()
        queue[c + DEPTH]()
        relay_each(c, start)
        if c - 1 in BENT:
            each(pass_left | pass_right, lambda: bend_own(c - 1, via_left), landed)
            pass_each(c - 1, start)

    def summarise():
        for copy in mid_copies:
            copy.wait_recv()
        fars[g] = dot(far_mean, mids[...].reshape(mid_raw, half)).astype(BF16)
        for copy in far_copies:
            copy.start()

    def collect():
        for copy in far_copies:
            copy.wait_recv()
        for i in range(2):
            picked = dot(pick(i, mid_place, mid_raw), mids[...].reshape(mid_raw, half))
            picked += dot(pick(i, far_place, far_raw), fars[...].reshape(far_raw, half))
            side[i] = picked.astype(BF16)

    def attend(c):
        x_copies(c)[2].wait_recv()
        recv = lambda copy: copy.wait_recv()
        each(even & has_right, lambda: own_copies(c, left), recv)
        each(odd & has_left, lambda: own_copies(c, right), recv)
        each(even & has_left, lambda: [relay_copy(c, right)], recv)
        each(odd & has_right, lambda: [relay_copy(c, left)], recv)
        for h in range(cw // head_dim):
            near_cols = pl.ds(c * cw + h * head_dim, head_dim)
            query = qs[:, :, near_cols].reshape(2 * BLOCK, head_dim)
            coarse = dot_t(query, side[0, :, near_cols]).reshape(mid_pair, MID_ROWS, side_count)
            coarse = jnp.sum(coarse, axis=1, keepdims=True) * (scale / MID_ROWS) + bias
            coarse = jnp.broadcast_to(coarse, (mid_pair, MID_ROWS, side_count))
            coarse = coarse.reshape(2 * BLOCK, side_count)
            for j in range(2):
                rows = slice(j * BLOCK, (j + 1) * BLOCK)
                keys = kv[0, j : j + 3, :, near_cols].reshape(3 * BLOCK, head_dim)
                vals = kv[1, j : j + 3, :, near_cols].reshape(3 * BLOCK, head_dim)
                values = jnp.concatenate([vals, side[1, :, near_cols]], axis=0)
                near = dot_t(query[rows], keys) * scale
                if j == 0:
                    edge = jnp.where(has_left, near[:, :BLOCK], -jnp.inf)
                    near = jnp.concatenate([edge, near[:, BLOCK:]], axis=1)
                else:
                    edge = jnp.where(has_right, near[:, 2 * BLOCK :], -jnp.inf)
                    near = jnp.concatenate([near[:, : 2 * BLOCK], edge], axis=1)
                scores = jnp.concatenate([near, coarse[rows]], axis=1)
                weight = jnp.exp(scores - jnp.max(scores, axis=1, keepdims=True))
                norm = jnp.sum(weight, axis=1, keepdims=True)
                numer = dot(weight.astype(BF16), values)
                outs[j, :, near_cols] = (numer * (1.0 / norm)).astype(BF16)
        out_remote(c).start()
        out_own(c).start()

    for c in range(CHUNKS):
        if c == CHUNKS // 2:
            summarise()
        if c == CHUNKS - 1:
            collect()
        arrive(c)
    local[4].wait()
    for c in range(CHUNKS):
        attend(c)

    sent = lambda copy: copy.wait_send()
    for copy in [rest_copy] + mid_copies + far_copies:
        copy.wait_send()
    for c in range(CHUNKS):
        for copy in x_copies(c):
            copy.wait_send()
        own_each(c, sent)
        relay_each(c, sent)
        if c in BENT:
            pass_each(c, sent)
        out_own(c).wait()
        out_remote(c).wait_send()
        out_remote(c).wait_recv()


def per_device(groups, seats, queries, keys, values):
    rows, width = queries.shape
    half = width // 2
    pairs = seats // 2
    mid_pair = 2 * BLOCK // MID_ROWS
    far_local = pairs * 2 * BLOCK // FAR_ROWS
    far_pad = -(-far_local // 8) * 8
    mid_count = pairs * mid_pair
    side_count = -(-(mid_count + groups * far_pad) // 128) * 128
    dma = pltpu.SemaphoreType.DMA
    peers = max(pairs - 1, 1)
    others = max(groups - 1, 1)
    return pl.pallas_call(
        functools.partial(kernel, groups, seats),
        out_shape=pltpu.VMEM((rows, width), BF16),
        in_specs=[pl.BlockSpec(memory_space=pl.ANY)] * 3,
        out_specs=pl.BlockSpec(memory_space=pltpu.VMEM),
        scratch_shapes=[
            pltpu.VMEM((2, 4, BLOCK, half), BF16),
            pltpu.VMEM((2, BLOCK, half), BF16),
            pltpu.VMEM((2, BLOCK, half), BF16),
            pltpu.VMEM((2, BLOCK, half), BF16),
            pltpu.VMEM((mid_pair, half), BF16),
            pltpu.VMEM((pairs, 2, mid_pair, half), BF16),
            pltpu.VMEM((groups, 2 * far_pad, half), BF16),
            pltpu.VMEM((2, side_count, half), BF16),
            pltpu.VMEM((2, BLOCK, half), BF16),
            dma((2, CHUNKS)),
            dma((2, CHUNKS)),
            dma((2, CHUNKS)),
            dma((5,)),
            dma(()),
            dma(()),
            dma((3, CHUNKS)),
            dma((3, CHUNKS)),
            dma((2, CHUNKS)),
            dma((2, CHUNKS)),
            dma((CHUNKS,)),
            dma((CHUNKS,)),
            dma((peers,)),
            dma((peers,)),
            dma((others,)),
            dma((others,)),
            dma((CHUNKS,)),
            dma((CHUNKS,)),
            dma((CHUNKS,)),
        ],
        compiler_params=pltpu.CompilerParams(collective_id=0, has_side_effects=True),
    )(queries, keys, values)


def solution(mesh):
    groups, seats = mesh.shape["grp"], mesh.shape["seq"]
    spec = P(("grp", "seq"), None)
    return jax.shard_map(
        functools.partial(per_device, groups, seats),
        mesh=mesh,
        in_specs=(spec, spec, spec),
        out_specs=spec,
        check_vma=False,
    )
```

```python
import functools
import math

import jax
import jax.numpy as jnp
from jax import lax
from jax.experimental import pallas as pl
from jax.experimental.pallas import tpu as pltpu
from jax.sharding import PartitionSpec as P

HEADS = 16
BLOCK = 128
MID_ROWS = 16
FAR_ROWS = 512
CHUNKS = 8
DEPTH = 2
BENT = tuple(range(0, CHUNKS - 1, 2))
MESH = pl.DeviceIdType.MESH
F32 = jnp.float32
BF16 = jnp.bfloat16


def dot(a, b):
    return lax.dot_general(a, b, (((1,), (0,)), ((), ())), preferred_element_type=F32)


def dot_t(a, b):
    return lax.dot_general(a, b, (((1,), (1,)), ((), ())), preferred_element_type=F32)


def kernel(
    groups,
    seats,
    q_ref,
    k_ref,
    v_ref,
    o_ref,
    kv,
    qs,
    outs,
    rest,
    rest_mid,
    mids,
    fars,
    side,
    bent,
    bent_send,
    bent_recv,
    pass_send,
    local_sem,
    rest_send,
    rest_recv,
    x_send,
    x_recv,
    own_send,
    own_recv,
    relay_send,
    relay_recv,
    mid_send,
    mid_recv,
    far_send,
    far_recv,
    out_send,
    out_recv,
    out_local,
):
    width = q_ref.shape[1]
    half = width // 2
    head_dim = width // HEADS
    cw = half // CHUNKS
    pairs = seats // 2
    total = groups * seats
    mid_pair = 2 * BLOCK // MID_ROWS
    mid_block = BLOCK // MID_ROWS
    mid_count = pairs * mid_pair
    far_local = mid_count * MID_ROWS // FAR_ROWS
    far_pad = fars.shape[1] // 2
    side_count = side.shape[1]
    scale = 1.0 / math.sqrt(head_dim)

    g = lax.axis_index("grp")
    s = lax.axis_index("seq")
    par = s % 2
    pair = s // 2
    place = g * seats + s
    mate = (g, s + 1 - 2 * par)
    left_place = (place + total - 2) % total
    right_place = (place + 2) % total
    left = (left_place // seats, left_place % seats)
    right = (right_place // seats, right_place % seats)
    has_left = place >= 2
    has_right = place < total - 2
    even = par == 0
    odd = par == 1
    mid_peers = [(g, (s + 2 * d) % seats) for d in range(1, pairs)]
    far_peers = [((g + d) % groups, s) for d in range(1, groups)]

    cross_left = (pair == 0) & has_left
    cross_right = (pair == pairs - 1) & has_right
    bend_left = cross_left & (g % 2 == 0)
    bend_right = cross_right & (g % 2 == 1)
    via_left = ((g + groups - 1) % groups, s)
    via_right = ((g + 1) % groups, s)
    pass_left = (pair == 0) & (g % 2 == 1) & (g < groups - 1)
    pass_right = (pair == pairs - 1) & (g % 2 == 0) & (g > 0)
    end_left = (g, (s + seats - 2) % seats)
    end_right = (g, (s + 2) % seats)

    barrier = pltpu.get_barrier_semaphore()

    def greet(device):
        pl.semaphore_signal(barrier, inc=1, device_id=device, device_id_type=MESH)

    for device in [mate] + mid_peers + far_peers:
        greet(device)
    pl.when(cross_left)(lambda: greet(left))
    pl.when(cross_right)(lambda: greet(right))

    mine = par * half
    theirs = half - mine

    def cols(base, c):
        return pl.ds(pl.multiple_of(base + c * cw, 128), cw)

    def cols_half(base):
        return pl.ds(pl.multiple_of(base, 128), half)

    def at(c):
        return pl.ds(c * cw, cw)

    local = []
    for i, (src, dst) in enumerate(
        [
            (k_ref.at[:, cols_half(mine)], kv.at[0, 1 + par]),
            (v_ref.at[:, cols_half(mine)], kv.at[1, 1 + par]),
            (k_ref.at[:, cols_half(theirs)], rest.at[0]),
            (v_ref.at[:, cols_half(theirs)], rest.at[1]),
            (q_ref.at[:, cols_half(mine)], qs.at[par]),
        ]
    ):
        local.append(pltpu.make_async_copy(src, dst, local_sem.at[i]))

    def remote(src, dst, send, recv, device):
        return pltpu.make_async_remote_copy(
            src_ref=src,
            dst_ref=dst,
            send_sem=send,
            recv_sem=recv,
            device_id=device,
            device_id_type=MESH,
        )

    def x_copies(c):
        targets = [
            (k_ref, kv.at[0, 1 + par, :, at(c)]),
            (v_ref, kv.at[1, 1 + par, :, at(c)]),
            (q_ref, qs.at[par, :, at(c)]),
        ]
        return [
            remote(src.at[:, cols(theirs, c)], dst, x_send.at[i, c], x_recv.at[i, c], mate)
            for i, (src, dst) in enumerate(targets)
        ]

    own_slot = 3 * (1 - par)
    relay_slot = 3 * par

    def own_copies(c, device):
        return [
            remote(
                src.at[:, cols(mine, c)],
                kv.at[i, own_slot, :, at(c)],
                own_send.at[i, c],
                own_recv.at[i, c],
                device,
            )
            for i, src in enumerate((k_ref, v_ref))
        ]

    def relay_copy(c, device):
        return remote(
            kv.at[:, 2 - par, :, at(c)],
            kv.at[:, relay_slot, :, at(c)],
            relay_send.at[c],
            relay_recv.at[c],
            device,
        )

    def bend_own(c, device):
        return [
            remote(
                src.at[:, cols(mine, c)],
                bent.at[i, :, at(c)],
                bent_send.at[i, c],
                bent_recv.at[i, c],
                device,
            )
            for i, src in enumerate((k_ref, v_ref))
        ]

    def bend_relay(c, device):
        return [
            remote(
                kv.at[i, 2 - par, :, at(c)],
                bent.at[i, :, at(c)],
                bent_send.at[i, c],
                bent_recv.at[i, c],
                device,
            )
            for i in range(2)
        ]

    def pass_own(c, device):
        return [
            remote(
                bent.at[i, :, at(c)],
                kv.at[i, own_slot, :, at(c)],
                pass_send.at[i, c],
                own_recv.at[i, c],
                device,
            )
            for i in range(2)
        ]

    def pass_relay(c, device):
        return remote(
            bent.at[:, :, at(c)],
            kv.at[:, relay_slot, :, at(c)],
            pass_send.at[0, c],
            relay_recv.at[c],
            device,
        )

    rest_copy = remote(rest_mid, mids.at[pair, par], rest_send, rest_recv, mate)
    mid_copies = [
        remote(mids.at[pair], mids.at[pair], mid_send.at[d], mid_recv.at[d], peer)
        for d, peer in enumerate(mid_peers)
    ]
    far_copies = [
        remote(fars.at[g], fars.at[g], far_send.at[d], far_recv.at[d], peer)
        for d, peer in enumerate(far_peers)
    ]

    def out_remote(c):
        return remote(
            outs.at[1 - par, :, at(c)],
            o_ref.at[:, cols(mine, c)],
            out_send.at[c],
            out_recv.at[c],
            mate,
        )

    def out_own(c):
        return pltpu.make_async_copy(
            outs.at[par, :, at(c)], o_ref.at[:, cols(mine, c)], out_local.at[c]
        )

    def each(cond, make, act):
        @pl.when(cond)
        def _():
            for copy in make():
                act(copy)

    def own_each(c, act):
        lefts, rights = even & has_left, odd & has_right
        if c in BENT:
            each(even & bend_left, lambda: bend_own(c, via_left), act)
            each(odd & bend_right, lambda: bend_own(c, via_right), act)
            lefts = lefts & jnp.logical_not(bend_left)
            rights = rights & jnp.logical_not(bend_right)
        each(lefts, lambda: own_copies(c, left), act)
        each(rights, lambda: own_copies(c, right), act)

    def relay_each(c, act):
        lefts, rights = odd & has_left, even & has_right
        if c in BENT:
            each(odd & bend_left, lambda: bend_relay(c, via_left), act)
            each(even & bend_right, lambda: bend_relay(c, via_right), act)
            lefts = lefts & jnp.logical_not(bend_left)
            rights = rights & jnp.logical_not(bend_right)
        each(rights, lambda: [relay_copy(c, right)], act)
        each(lefts, lambda: [relay_copy(c, left)], act)

    def pass_each(c, act):
        each(even & pass_left, lambda: pass_own(c, end_left), act)
        each(odd & pass_right, lambda: pass_own(c, end_right), act)
        each(odd & pass_left, lambda: [pass_relay(c, end_left)], act)
        each(even & pass_right, lambda: [pass_relay(c, end_right)], act)

    for copy in local:
        copy.start()

    @pl.when(jnp.logical_not(has_left))
    def _():
        kv[:, 0] = jnp.zeros((2, BLOCK, half), BF16)

    @pl.when(jnp.logical_not(has_right))
    def _():
        kv[:, 3] = jnp.zeros((2, BLOCK, half), BF16)

    def table(rows, columns):
        shape = (rows, columns)
        return (
            lax.broadcasted_iota(jnp.int32, shape, 0),
            lax.broadcasted_iota(jnp.int32, shape, 1),
        )

    row, col = table(mid_pair, 2 * BLOCK)
    mid_mean = jnp.where(col // MID_ROWS == row, 1.0 / MID_ROWS, 0.0).astype(BF16)
    for copy in local[:4]:
        copy.wait()
    mids[pair, par] = dot(mid_mean, kv[:, 1 + par].reshape(2 * BLOCK, half)).astype(BF16)
    rest_mid[...] = dot(mid_mean, rest[...].reshape(2 * BLOCK, half)).astype(BF16)

    crossing = cross_left.astype(jnp.int32) + cross_right.astype(jnp.int32)
    pl.semaphore_wait(barrier, 1 + len(mid_peers) + len(far_peers) + crossing)

    start = lambda copy: copy.start()
    start = lambda copy: copy.start()

    def push_pair(c):
        own_each(c, start)
        for copy in x_copies(c)[:2]:
            copy.start()

    queue = [functools.partial(push_pair, c) for c in range(CHUNKS)]
    batch = CHUNKS // DEPTH
    for b in range(DEPTH):
        queue.append(
            lambda b=b: [x_copies(c)[2].start() for c in range(b * batch, (b + 1) * batch)]
        )
    rest_copy.start()
    for push in queue[:DEPTH]:
        push()
    rest_copy.wait_recv()
    for copy in mid_copies:
        copy.start()

    mid_raw = pairs * 2 * mid_pair
    far_raw = groups * 2 * far_pad
    ratio = FAR_ROWS // MID_ROWS

    def mid_place(raw):
        return raw // (2 * mid_block) * mid_block + raw % mid_block, raw // mid_block % 2

    def far_place(raw):
        return raw // (2 * far_pad) * far_pad + raw % far_pad + mid_count, raw // far_pad % 2

    row, col = table(2 * far_pad, mid_raw)
    index, kind = mid_place(col)
    far_hit = (index // ratio == row % far_pad) & (kind == row // far_pad)
    far_mean = jnp.where(far_hit, 1.0 / ratio, 0.0).astype(BF16)

    def pick(kind, place, raw):
        row, col = table(side_count, raw)
        index, found = place(col)
        return jnp.where((index == row) & (found == kind), 1.0, 0.0).astype(BF16)

    shape = (mid_pair, 1, side_count)
    query_block = 2 * pair + lax.broadcasted_iota(jnp.int32, shape, 0) // mid_block
    index = lax.broadcasted_iota(jnp.int32, shape, 2)
    far_index = index - mid_count
    mid_ok = (index < mid_count) & (jnp.abs(index // mid_block - query_block) > 1)
    far_ok = (far_index >= 0) & (far_index < groups * far_pad)
    far_ok = far_ok & (far_index // far_pad != g) & (far_index % far_pad < far_local)
    bias = jnp.where(mid_ok | far_ok, 0.0, -jnp.inf)

    landed = lambda copy: copy.wait_recv()

    def arrive(c):
        for copy in x_copies(c)[:2]:
            copy.wait_recv()
        relay_each(c, start)
        queue[c + DEPTH]()
        if c - 1 in BENT:
            each(pass_left | pass_right, lambda: bend_own(c - 1, via_left), landed)
            pass_each(c - 1, start)

    def summarise():
        for copy in mid_copies:
            copy.wait_recv()
        fars[g] = dot(far_mean, mids[...].reshape(mid_raw, half)).astype(BF16)
        for copy in far_copies:
            copy.start()

    def collect():
        for copy in far_copies:
            copy.wait_recv()
        for i in range(2):
            picked = dot(pick(i, mid_place, mid_raw), mids[...].reshape(mid_raw, half))
            picked += dot(pick(i, far_place, far_raw), fars[...].reshape(far_raw, half))
            side[i] = picked.astype(BF16)

    def attend(c):
        x_copies(c)[2].wait_recv()
        recv = lambda copy: copy.wait_recv()
        each(even & has_right, lambda: own_copies(c, left), recv)
        each(odd & has_left, lambda: own_copies(c, right), recv)
        each(even & has_left, lambda: [relay_copy(c, right)], recv)
        each(odd & has_right, lambda: [relay_copy(c, left)], recv)
        for h in range(cw // head_dim):
            near_cols = pl.ds(c * cw + h * head_dim, head_dim)
            query = qs[:, :, near_cols].reshape(2 * BLOCK, head_dim)
            coarse = dot_t(query, side[0, :, near_cols]).reshape(mid_pair, MID_ROWS, side_count)
            coarse = jnp.sum(coarse, axis=1, keepdims=True) * (scale / MID_ROWS) + bias
            coarse = jnp.broadcast_to(coarse, (mid_pair, MID_ROWS, side_count))
            coarse = coarse.reshape(2 * BLOCK, side_count)
            for j in range(2):
                rows = slice(j * BLOCK, (j + 1) * BLOCK)
                keys = kv[0, j : j + 3, :, near_cols].reshape(3 * BLOCK, head_dim)
                vals = kv[1, j : j + 3, :, near_cols].reshape(3 * BLOCK, head_dim)
                values = jnp.concatenate([vals, side[1, :, near_cols]], axis=0)
                near = dot_t(query[rows], keys) * scale
                if j == 0:
                    edge = jnp.where(has_left, near[:, :BLOCK], -jnp.inf)
                    near = jnp.concatenate([edge, near[:, BLOCK:]], axis=1)
                else:
                    edge = jnp.where(has_right, near[:, 2 * BLOCK :], -jnp.inf)
                    near = jnp.concatenate([near[:, : 2 * BLOCK], edge], axis=1)
                scores = jnp.concatenate([near, coarse[rows]], axis=1)
                weight = jnp.exp(scores - jnp.max(scores, axis=1, keepdims=True))
                norm = jnp.sum(weight, axis=1, keepdims=True)
                numer = dot(weight.astype(BF16), values)
                outs[j, :, near_cols] = (numer * (1.0 / norm)).astype(BF16)
        out_remote(c).start()
        out_own(c).start()

    for c in range(CHUNKS):
        if c == CHUNKS // 2:
            summarise()
        if c == CHUNKS - 1:
            collect()
        arrive(c)
    local[4].wait()
    for c in range(CHUNKS):
        attend(c)

    sent = lambda copy: copy.wait_send()
    for copy in [rest_copy] + mid_copies + far_copies:
        copy.wait_send()
    for c in range(CHUNKS):
        for copy in x_copies(c):
            copy.wait_send()
        own_each(c, sent)
        relay_each(c, sent)
        if c in BENT:
            pass_each(c, sent)
        out_own(c).wait()
        out_remote(c).wait_send()
        out_remote(c).wait_recv()


def per_device(groups, seats, queries, keys, values):
    rows, width = queries.shape
    half = width // 2
    pairs = seats // 2
    mid_pair = 2 * BLOCK // MID_ROWS
    far_local = pairs * 2 * BLOCK // FAR_ROWS
    far_pad = -(-far_local // 8) * 8
    mid_count = pairs * mid_pair
    side_count = -(-(mid_count + groups * far_pad) // 128) * 128
    dma = pltpu.SemaphoreType.DMA
    peers = max(pairs - 1, 1)
    others = max(groups - 1, 1)
    return pl.pallas_call(
        functools.partial(kernel, groups, seats),
        out_shape=pltpu.VMEM((rows, width), BF16),
        in_specs=[pl.BlockSpec(memory_space=pl.ANY)] * 3,
        out_specs=pl.BlockSpec(memory_space=pltpu.VMEM),
        scratch_shapes=[
            pltpu.VMEM((2, 4, BLOCK, half), BF16),
            pltpu.VMEM((2, BLOCK, half), BF16),
            pltpu.VMEM((2, BLOCK, half), BF16),
            pltpu.VMEM((2, BLOCK, half), BF16),
            pltpu.VMEM((mid_pair, half), BF16),
            pltpu.VMEM((pairs, 2, mid_pair, half), BF16),
            pltpu.VMEM((groups, 2 * far_pad, half), BF16),
            pltpu.VMEM((2, side_count, half), BF16),
            pltpu.VMEM((2, BLOCK, half), BF16),
            dma((2, CHUNKS)),
            dma((2, CHUNKS)),
            dma((2, CHUNKS)),
            dma((5,)),
            dma(()),
            dma(()),
            dma((3, CHUNKS)),
            dma((3, CHUNKS)),
            dma((2, CHUNKS)),
            dma((2, CHUNKS)),
            dma((CHUNKS,)),
            dma((CHUNKS,)),
            dma((peers,)),
            dma((peers,)),
            dma((others,)),
            dma((others,)),
            dma((CHUNKS,)),
            dma((CHUNKS,)),
            dma((CHUNKS,)),
        ],
        compiler_params=pltpu.CompilerParams(collective_id=0, has_side_effects=True),
    )(queries, keys, values)


def solution(mesh):
    groups, seats = mesh.shape["grp"], mesh.shape["seq"]
    spec = P(("grp", "seq"), None)
    return jax.shard_map(
        functools.partial(per_device, groups, seats),
        mesh=mesh,
        in_specs=(spec, spec, spec),
        out_specs=spec,
        check_vma=False,
    )
```
